512 devices in a mesh: row: 16 (over x, y), col: 16 (over z_lo, core), depth: 2 (over z_hi).
Axes of the slice: x: 4, y: 4, z: 16 (z_hi: 2, z_lo: 8; z = z_hi * 8 + z_lo), core: 2. Of those that a mesh axis runs over, the one named last changes fastest.
Arguments:
- grad_out: bfloat16 [65536, 512], P(('row', 'col', 'depth')), may hold values from -6 to 6
- relu_mask: int32 [65536, 512], P(('row', 'col', 'depth')), may hold values 0 or 1
- aggregated: bfloat16 [65536, 512], P(('row', 'col', 'depth')), may hold values from -0.0234375 to 0.0234375
- weight: bfloat16 [512, 512], replicated, may hold values from -0.25 to 0.25
- adjacency_tiles: bfloat16 [43008, 128, 128], P(('row', 'col', 'depth')), may hold values from -0.09375 to 0.09375
- tile_rows: int32 [43008], P(('row', 'col', 'depth')), may hold values from 0 to 15
- tile_cols: int32 [43008], P(('row', 'col', 'depth')), may hold values from 0 to 31
- tile_count: int32 [512], P(('row', 'col', 'depth')), may hold values from 10 to 84, as said below
Outputs:
- node_grad: bfloat16 [65536, 512], P(('row', 'col', 'depth'))
- weight_grad: float32 [512, 512], replicated
The draws below stay inside these ranges and needn't reach their ends.
Inputs may be any that keep to these rules, and one draw needn't show every extreme that they name: `tile_count`: some device has all 84 slots live in every draw; most have far fewer.
All inputs are finite; a program needn't handle non-finite values. No bound on the sum of `relu_mask` on one device may be relied on, other than what follows from the above.
Results may differ from the reference program's by a relative error of at most 0.024.
Values may be sent and summed in bfloat16 or wider, within the bound.
A program may use at most 64 MiB of HBM per device.

```python
import jax
import jax.numpy as jnp
from jax import lax

F = 512
TILE = 128
ROWS_DEV = 128
TILES_DEV = 84
SHARDS = 512
SOURCES = 32
NODES = 65536
TILES = 43008
SLAB_TILES = 16
GROUP_TILES = 32
N_ROW = 16
N_COL = 16
N_DEPTH = 2


def draw_tile_count(key, part):
    key = jax.random.fold_in(key, 7)
    first, second, third = jax.random.split(key, 3)
    lighter = jax.random.randint(first, (SHARDS,), TILES_DEV // 8, TILES_DEV // 2 + 1)
    heavier = jax.random.randint(second, (SHARDS,), 0, 8) == 0
    counts = jnp.where(heavier, TILES_DEV, lighter)
    forced = jax.random.randint(third, (), 0, SHARDS)
    counts = counts.at[forced].set(TILES_DEV)
    return counts.astype(jnp.int32)


def with_ends(drawn, stream_key, least, top_value):
    place = [jax.random.randint(jax.random.fold_in(stream_key, axis), (), 0, length) for axis, length in enumerate(drawn.shape)]
    widest = drawn.shape.index(max(drawn.shape))
    beside = place[:widest] + [(place[widest] + 1) % drawn.shape[widest]] + place[widest + 1:]
    return drawn.at[tuple(place)].set(least).at[tuple(beside)].set(top_value)


def levels(stream_key, dims, pieces, smallest, high):
    loudness = 1.0
    for dim, parts in pieces:
        heights = jax.random.uniform(jax.random.fold_in(jax.random.fold_in(stream_key, 6), dim), (parts,), jnp.float32, smallest / len(pieces), high / len(pieces))
        loudness = loudness * jnp.repeat(jnp.exp(heights), dims[dim] // parts).reshape((-1,) + (1,) * (len(dims) - 1 - dim))
    return loudness


def centred(own_key, shape, scale, most, shards=(), held_as=jnp.bfloat16):
    values = jax.random.normal(own_key, shape, jnp.float32) * scale
    if len(shards) > 0:
        values = levels(own_key, shape, shards, -0.22, 0.18) * values
    return jnp.clip(values, min=-most, max=most).astype(held_as)


def setup_inputs(seed: int = 0) -> dict:
    arg_keys = jax.random.split(jax.random.key(seed), 9)
    grad_out = centred(arg_keys[0], (NODES, F), 1.0, 6.0, ((0, 512),))
    relu_mask = with_ends((jax.random.randint(arg_keys[1], (NODES, F), 0, 2) < 1).astype(jnp.int32), jax.random.fold_in(arg_keys[1], 1), 0, 1)
    aggregated = centred(arg_keys[2], (NODES, F), NODES ** -0.5, 0.0234375, ((0, 512),))
    weight = centred(arg_keys[3], (F, F), F ** -0.5, 0.25)
    adjacency_tiles = centred(arg_keys[4], (TILES, TILE, TILE), (TILE * SOURCES) ** -0.5, 0.09375, ((0, 512),))
    tile_rows = with_ends(jax.random.randint(arg_keys[5], (TILES,), 0, SLAB_TILES), jax.random.fold_in(arg_keys[5], 1), 0, SLAB_TILES - 1).astype(jnp.int32)
    tile_cols = with_ends(jax.random.randint(arg_keys[6], (TILES,), 0, GROUP_TILES), jax.random.fold_in(arg_keys[6], 1), 0, GROUP_TILES - 1).astype(jnp.int32)
    tile_count = draw_tile_count(jax.random.fold_in(arg_keys[8], 71), 0)
    return {"grad_out": grad_out, "relu_mask": relu_mask, "aggregated": aggregated, "weight": weight, "adjacency_tiles": adjacency_tiles, "tile_rows": tile_rows, "tile_cols": tile_cols, "tile_count": tile_count}


def reference(grad_out, relu_mask, aggregated, weight, adjacency_tiles, tile_rows, tile_cols, tile_count):
    grad_pre = grad_out * relu_mask.astype(jnp.bfloat16)
    weight_grad = jnp.dot(aggregated.T, grad_pre, preferred_element_type=jnp.float32)
    projected = jnp.dot(grad_pre, weight.T, preferred_element_type=jnp.float32).astype(jnp.bfloat16)
    projected_grid = projected.reshape(N_ROW, N_COL, N_DEPTH, ROWS_DEV, F)
    tile_grid = adjacency_tiles.reshape(SHARDS, TILES_DEV, TILE, TILE)
    row_grid = tile_rows.reshape(SHARDS, TILES_DEV)
    col_grid = tile_cols.reshape(SHARDS, TILES_DEV)

    def shard_term(shard_index, total):
        row_pos = shard_index // (N_COL * N_DEPTH)
        col_pos = (shard_index // N_DEPTH) % N_COL
        depth_pos = shard_index % N_DEPTH
        by_row = lax.dynamic_index_in_dim(projected_grid, row_pos, 0, keepdims=False)
        panel = lax.dynamic_index_in_dim(by_row, depth_pos, 1, keepdims=False)
        panel = panel.reshape(SLAB_TILES, TILE, F)
        alive = (jnp.arange(TILES_DEV) < tile_count[shard_index]).astype(jnp.float32)
        picked = panel[row_grid[shard_index]].astype(jnp.float32)
        chosen = tile_grid[shard_index].astype(jnp.float32) * alive[:, None, None]
        products = jnp.einsum("kab,kaf->kbf", chosen, picked)
        partial_value = jnp.zeros((GROUP_TILES, TILE, F), jnp.float32).at[col_grid[shard_index]].add(products)
        rounded = lax.optimization_barrier(partial_value.astype(jnp.bfloat16)).astype(jnp.float32)
        rounded = rounded.reshape(N_ROW, N_DEPTH, ROWS_DEV, F)
        column = lax.dynamic_index_in_dim(total, col_pos, 1, keepdims=False)
        return lax.dynamic_update_index_in_dim(total, column + rounded, col_pos, 1)

    start_total = jnp.zeros((N_ROW, N_COL, N_DEPTH, ROWS_DEV, F), jnp.float32)
    total = lax.fori_loop(0, SHARDS, shard_term, start_total)
    node_grad = total.reshape(NODES, F).astype(jnp.bfloat16)
    return node_grad, weight_grad
```

```python
import jax
import jax.numpy as jnp
from jax import lax
from jax.experimental import pallas as pl
from jax.experimental.pallas import tpu as pltpu
from jax.sharding import PartitionSpec as P

MESH = pl.DeviceIdType.MESH
F32 = jnp.float32
BF16 = jnp.bfloat16
T = 128
NCHUNK = 4
SLOTS = 84
GROUP = 32
UNROLL = 6
HALF = SLOTS // 2
SEMS = 320


def wrap4(value):
    return lax.rem(value, 4)


class Ring:
    def __init__(self, k, src, unit, rl, rr, fl, fr, out, right, left):
        self.src, self.unit, self.out = src, unit, out
        self.rl, self.rr, self.fl, self.fr = rl, rr, fl, fr
        u = unit
        self.to_right = k.copy(src.at[pl.ds(3 * u, 2 * u)], rl, right)
        self.to_left = k.copy(src.at[pl.ds(5 * u, 2 * u)], rr, left)
        self.sum_right = k.copy(src.at[pl.ds(2 * u, u)], fl, right)
        self.sum_left = k.copy(src.at[pl.ds(7 * u, u)], fr, left)

    def first(self):
        self.to_right.start()
        self.to_left.start()

    def second(self):
        u, src = self.unit, self.src
        self.to_right.wait_recv()
        src[pl.ds(2 * u, u)] = (
            src[pl.ds(2 * u, u)].astype(F32) + self.rl[pl.ds(u, u)].astype(F32)
        ).astype(BF16)
        self.sum_right.start()
        self.to_left.wait_recv()
        src[pl.ds(7 * u, u)] = (
            src[pl.ds(7 * u, u)].astype(F32) + self.rr[pl.ds(0, u)].astype(F32)
        ).astype(BF16)
        self.sum_left.start()

    def last(self):
        u, src = self.unit, self.src
        self.sum_right.wait_recv()
        self.out[pl.ds(0, u)] = (
            src[pl.ds(0, u)].astype(F32)
            + self.fl[...].astype(F32)
            + self.rr[pl.ds(u, u)].astype(F32)
        ).astype(BF16)
        self.sum_left.wait_recv()
        self.out[pl.ds(u, u)] = (
            src[pl.ds(u, u)].astype(F32)
            + self.rl[pl.ds(0, u)].astype(F32)
            + self.fr[...].astype(F32)
        ).astype(BF16)


class Copies:
    def __init__(self, send_sems, recv_sems):
        self.send_sems, self.recv_sems, self.used = send_sems, recv_sems, 0
        self.all = []

    def copy(self, src, dst, device):
        index = self.used
        self.used += 1
        made = pltpu.make_async_remote_copy(
            src_ref=src,
            dst_ref=dst,
            send_sem=self.send_sems.at[index],
            recv_sem=self.recv_sems.at[index],
            device_id=device,
            device_id_type=MESH,
        )
        self.all.append(made)
        return made


def kernel(
    order_ref, gate_ref, grad_ref, mask_ref, agg_ref, weight_ref, tiles_hbm,
    node_ref, wgrad_ref,
    tiles, seg, acc_ref,
    g0, g1, g2, g3,
    parts, xl, xr, xfl, xfr, mids, yl, yr, yfl, yfr, tops, ztop,
    wl, ws, wa, wxl, wxr, wxfl, wxfr, wb, wyl, wyr, wyfl, wyfr, wc, wz, wg,
    send_sems, recv_sems, tile_sem,
):
    row, col, depth = lax.axis_index("row"), lax.axis_index("col"), lax.axis_index("depth")
    x, y = lax.div(row, 4), lax.rem(row, 4)
    z, core = lax.div(col, 2), lax.rem(col, 2)
    zz = depth * 8 + z
    gathered = (g0, g1, g2, g3)

    def device(dx=0, dy=0):
        return (wrap4(x + dx) * 4 + wrap4(y + dy), col, depth)

    def along_z(step):
        place = lax.rem(zz + step, 16)
        return (row, lax.rem(place, 8) * 2 + core, lax.div(place, 8)), place

    def along_group(step):
        place = lax.rem(z + step, 8)
        return (row, place * 2 + core, depth), place

    sibling = (row, z * 2 + 1 - core, depth)
    right_x, left_x = device(dx=1), device(dx=3)
    right_y, left_y = device(dy=1), device(dy=3)
    partner = (row, col, 1 - depth)
    k = Copies(send_sems, recv_sems)

    load_tiles = pltpu.make_async_copy(tiles_hbm, tiles, tile_sem)
    load_tiles.start()

    barrier = pltpu.get_barrier_semaphore()
    peers = [sibling] + [device(dx=s) for s in (1, 2, 3)] + [device(dy=s) for s in (1, 2, 3)]
    peers += [along_z(s)[0] for s in range(1, 16)]
    for peer in peers:
        pl.semaphore_signal(barrier, inc=1, device_id=peer, device_id_type=MESH)

    grad = grad_ref[...] * mask_ref[...].astype(F32).astype(BF16)
    own = core * 8 + z
    for c in range(NCHUNK):
        gathered[c][own] = lax.dot_general(
            weight_ref[pl.ds(c * T, T), :], grad, (((1,), (1,)), ((), ())),
            preferred_element_type=F32,
        ).astype(BF16)
    pl.semaphore_wait(barrier, len(peers))

    spread, arrive, share = [], [], []
    for c in range(NCHUNK):
        sends, comes = [], []
        for step in range(1, 8):
            target, _ = along_group(step)
            sent = k.copy(gathered[c].at[own], gathered[c].at[own], target)
            sends.append(sent)
            _, source = along_group(8 - step)
            slot = gathered[c].at[core * 8 + source]
            comes.append(
                pltpu.make_async_remote_copy(
                    src_ref=slot, dst_ref=slot,
                    send_sem=send_sems.at[k.used - 1], recv_sem=recv_sems.at[k.used - 1],
                    device_id=target, device_id_type=MESH,
                )
            )
        spread.append(sends)
        arrive.append(comes)
        mine = gathered[c].at[pl.ds(core * 8, 8)]
        share.append(k.copy(mine, mine, sibling))

    def gather_start(c):
        for sent in spread[c]:
            sent.start()

    def gather_pass(c):
        for came in arrive[c]:
            came.wait_recv()
        share[c].start()

    def gather_done(c):
        share[c].wait_recv()

    gather_start(0)
    gather_start(1)

    for h in range(2):
        for q in range(4):
            wl[h, q] = lax.dot_general(
                agg_ref[:, h * 256:(h + 1) * 256], grad[:, q * T:(q + 1) * T],
                (((0,), (0,)), ((), ())), preferred_element_type=F32,
            ).astype(BF16)
    w_share = k.copy(wl.at[1 - core], ws, sibling)
    w_share.start()
    w_x = Ring(k, wa, 128, wxl, wxr, wxfl, wxfr, wb, right_x, left_x)
    w_y = Ring(k, wb, 32, wyl, wyr, wyfl, wyfr, wc, right_y, left_y)
    w_z = []
    w_z_comes = []
    for step in range(1, 16):
        target, _ = along_z(step)
        _, source = along_z(16 - step)
        w_z.append(k.copy(wz.at[zz], wz.at[zz], target))
        w_z_comes.append(
            pltpu.make_async_remote_copy(
                src_ref=wz.at[source], dst_ref=wz.at[source],
                send_sem=send_sems.at[k.used - 1], recv_sem=recv_sems.at[k.used - 1],
                device_id=target, device_id_type=MESH,
            )
        )
    w_back_y, w_back_y_comes, w_back_x, w_back_x_comes = [], [], [], []
    for step in range(1, 4):
        block = wg.at[core, x, y]
        w_back_y.append(k.copy(block, block, device(dy=step)))
        came = wg.at[core, x, wrap4(y + 4 - step)]
        w_back_y_comes.append(
            pltpu.make_async_remote_copy(
                src_ref=came, dst_ref=came,
                send_sem=send_sems.at[k.used - 1], recv_sem=recv_sems.at[k.used - 1],
                device_id=device(dy=step), device_id_type=MESH,
            )
        )
    for step in range(1, 4):
        block = wg.at[core, x]
        w_back_x.append(k.copy(block, block, device(dx=step)))
        came = wg.at[core, wrap4(x + 4 - step)]
        w_back_x_comes.append(
            pltpu.make_async_remote_copy(
                src_ref=came, dst_ref=came,
                send_sem=send_sems.at[k.used - 1], recv_sem=recv_sems.at[k.used - 1],
                device_id=device(dx=step), device_id_type=MESH,
            )
        )
    w_back_core = k.copy(wg.at[core], wg.at[core], sibling)
    w_back_core_came = pltpu.make_async_remote_copy(
        src_ref=wg.at[1 - core], dst_ref=wg.at[1 - core],
        send_sem=send_sems.at[k.used - 1], recv_sem=recv_sems.at[k.used - 1],
        device_id=sibling, device_id_type=MESH,
    )

    def weight_1():
        w_share.wait_recv()
        for a in range(4):
            xt = wrap4(x + a)
            for b in range(4):
                rows = pl.ds(pl.multiple_of(wrap4(y + b) * 64, 64), 64)
                wa[pl.ds(a * 256 + b * 64, 64)] = (
                    wl[core, xt, rows].astype(F32) + ws[xt, rows].astype(F32)
                ).astype(BF16)
        w_x.first()

    def weight_3():
        w_x.last()
        w_y.first()

    def weight_5():
        w_y.last()
        wz[zz] = wc[...]
        for sent in w_z:
            sent.start()

    def weight_6():
        for came in w_z_comes:
            came.wait_recv()
        total = wz[0].astype(F32)
        for place in range(1, 16):
            total = total + wz[place].astype(F32)
        wg[core, x, y] = total.astype(BF16)
        for sent in w_back_y:
            sent.start()

    def weight_7():
        for came in w_back_y_comes:
            came.wait_recv()
        for sent in w_back_x:
            sent.start()

    def weight_8():
        for came in w_back_x_comes:
            came.wait_recv()
        w_back_core.start()

    def weight_9():
        w_back_core_came.wait_recv()
        wgrad_ref[...] = wg[...]

    def compute(c, first, stop):
        def block(step, acc):
            for inner in range(UNROLL):
                p = first + step * UNROLL + inner
                product = jnp.dot(
                    gathered[c][order_ref[1, p]], tiles[order_ref[0, p]],
                    preferred_element_type=F32,
                )
                acc = acc * gate_ref[0, p] + product
                seg[p] = acc.astype(BF16)
            return acc

        if first == 0:
            start = jnp.zeros((T, T), F32)
        else:
            start = acc_ref[...]
        end = lax.fori_loop(0, (stop - first) // UNROLL, block, start)
        if stop < SLOTS:
            acc_ref[...] = end

    def place(c):
        def one(m, carry):
            major, minor = lax.div(m, 4), lax.rem(m, 4)
            rows = pl.ds(pl.multiple_of(m * T, T), T)
            for dt in range(2):
                a, b = (major, minor) if dt == 0 else (minor, major)
                target = (wrap4(x + a) * 4 + wrap4(y + b)) * 2 + dt
                parts[c, dt, rows] = (
                    seg[order_ref[2, target]].astype(F32) * gate_ref[1, target]
                ).astype(BF16)
            return carry

        lax.fori_loop(0, 16, one, 0)

    ring_a, ring_b, cross = [], [], []
    for c in range(NCHUNK):
        for dt in range(2):
            far = (right_x, left_x) if dt == 0 else (right_y, left_y)
            near = (right_y, left_y) if dt == 0 else (right_x, left_x)
            ring_a.append(Ring(
                k, parts.at[c, dt], 256, xl.at[c, dt], xr.at[c, dt], xfl.at[c, dt], xfr.at[c, dt],
                mids.at[c, dt], *far,
            ))
            ring_b.append(Ring(
                k, mids.at[c, dt], 64, yl.at[c, dt], yr.at[c, dt], yfl.at[c, dt], yfr.at[c, dt],
                tops.at[c, dt], *near,
            ))
        cross.append(k.copy(tops.at[c, 1 - depth], ztop.at[c], partner))

    def reduce_1(c):
        for dt in range(2):
            ring_a[2 * c + dt].first()

    def reduce_2(c):
        for dt in range(2):
            ring_a[2 * c + dt].second()

    def reduce_3(c):
        for dt in range(2):
            ring_a[2 * c + dt].last()
            ring_b[2 * c + dt].first()

    def reduce_4(c):
        for dt in range(2):
            ring_b[2 * c + dt].second()

    def reduce_5(c):
        for dt in range(2):
            ring_b[2 * c + dt].last()
        cross[c].start()

    def reduce_6(c):
        cross[c].wait_recv()
        node_ref[pl.ds(c * T, T)] = (
            tops[c, depth].astype(F32) + ztop[c].astype(F32)
        ).astype(BF16)

    gather_pass(0)
    gather_start(2)
    weight_1()
    load_tiles.wait()
    gather_done(0)
    compute(0, 0, HALF)
    w_x.second()
    compute(0, HALF, SLOTS)
    place(0)
    reduce_1(0)

    gather_pass(1)
    gather_start(3)
    weight_3()
    gather_done(1)
    compute(1, 0, HALF)
    reduce_2(0)
    w_y.second()
    compute(1, HALF, SLOTS)
    place(1)
    reduce_1(1)

    reduce_3(0)
    gather_pass(2)
    weight_5()
    gather_done(2)
    compute(2, 0, HALF)
    reduce_2(1)
    reduce_4(0)
    compute(2, HALF, SLOTS)
    place(2)
    reduce_1(2)

    reduce_3(1)
    reduce_5(0)
    gather_pass(3)
    weight_6()
    gather_done(3)
    compute(3, 0, HALF)
    reduce_2(2)
    reduce_4(1)
    compute(3, HALF, SLOTS)
    place(3)
    reduce_1(3)

    weight_7()
    reduce_3(2)
    reduce_5(1)
    reduce_6(0)
    reduce_2(3)
    reduce_4(2)
    weight_8()
    reduce_3(3)
    reduce_5(2)
    reduce_6(1)
    reduce_4(3)
    reduce_6(2)
    reduce_5(3)
    weight_9()
    reduce_6(3)
    for made in k.all:
        made.wait_send()


def on_device(
    grad_out, relu_mask, aggregated, weight, adjacency_tiles, tile_rows, tile_cols, tile_count
):
    slots = jnp.arange(SLOTS)
    key = jnp.where(slots < tile_count[0], tile_cols, GROUP)
    before = (key[None, :] < key[:, None]) | (
        (key[None, :] == key[:, None]) & (slots[None, :] < slots[:, None])
    )
    rank = jnp.sum(before.astype(jnp.int32), axis=1)
    picked = (rank[None, :] == slots[:, None]).astype(jnp.int32)
    order = jnp.sum(picked * slots[None, :], axis=1)
    place = (tile_rows % 2) * 8 + tile_rows // 2
    rows = jnp.sum(picked * place[None, :], axis=1)
    starts = jnp.sum(picked * jnp.sum(
        ((key[None, :] == key[:, None]) & (slots[None, :] < slots[:, None])).astype(jnp.int32), axis=1
    )[None, :], axis=1)
    keep = (starts > 0).astype(F32)
    groups = jnp.arange(SLOTS)
    upto = jnp.sum((key[None, :] <= groups[:, None]).astype(jnp.int32), axis=1)
    last = jnp.maximum(upto - 1, 0)
    has = jnp.max((key[None, :] == groups[:, None]).astype(F32), axis=1)
    order_all = jnp.stack([order, rows, last])
    gates = jnp.stack([keep, has])

    smem = pl.BlockSpec(memory_space=pltpu.SMEM)
    vmem = pl.BlockSpec(memory_space=pltpu.VMEM)
    bf = lambda *shape: pltpu.VMEM(shape, BF16)
    node_t, wgrad = pl.pallas_call(
        kernel,
        out_shape=(
            jax.ShapeDtypeStruct((NCHUNK * T, T), BF16),
            jax.ShapeDtypeStruct((2, 4, 4, 64, T), BF16),
        ),
        in_specs=[smem, smem, vmem, vmem, vmem, vmem, pl.BlockSpec(memory_space=pl.ANY)],
        out_specs=(vmem, vmem),
        scratch_shapes=[
            bf(SLOTS, T, T), bf(SLOTS, T, T), pltpu.VMEM((T, T), F32),
            bf(16, T, T), bf(16, T, T), bf(16, T, T), bf(16, T, T),
            bf(4, 2, 16 * T, T),
            bf(4, 2, 512, T), bf(4, 2, 512, T), bf(4, 2, 256, T), bf(4, 2, 256, T),
            bf(4, 2, 512, T),
            bf(4, 2, 128, T), bf(4, 2, 128, T), bf(4, 2, 64, T), bf(4, 2, 64, T),
            bf(4, 2, 128, T), bf(4, 128, T),
            bf(2, 4, 256, T), bf(4, 256, T), bf(1024, T),
            bf(256, T), bf(256, T), bf(128, T), bf(128, T),
            bf(256, T),
            bf(64, T), bf(64, T), bf(32, T), bf(32, T),
            bf(64, T), bf(16, 64, T), bf(2, 4, 4, 64, T),
            pltpu.SemaphoreType.DMA((SEMS,)),
            pltpu.SemaphoreType.DMA((SEMS,)),
            pltpu.SemaphoreType.DMA,
        ],
        compiler_params=pltpu.CompilerParams(
            collective_id=0, has_side_effects=True, vmem_limit_bytes=48 * 1024 * 1024
        ),
        cost_estimate=pl.CostEstimate(flops=1_600_000_000, bytes_accessed=5_000_000, transcendentals=0),
    )(order_all, gates, grad_out, relu_mask, aggregated, weight, adjacency_tiles)
    node_grad = node_t.T
    weight_grad = wgrad.transpose(0, 2, 3, 1, 4).reshape(512, 512).astype(F32)
    return (node_grad, weight_grad)


def solution(mesh):
    return jax.shard_map(
        on_device,
        mesh=mesh,
        in_specs=(
            P(("row", "col", "depth"), None),
            P(("row", "col", "depth"), None),
            P(("row", "col", "depth"), None),
            P(),
            P(("row", "col", "depth"), None, None),
            P(("row", "col", "depth")),
            P(("row", "col", "depth")),
            P(("row", "col", "depth")),
        ),
        out_specs=(P(("row", "col", "depth"), None), P()),
        check_vma=False,
    )
```

```python
import jax
import jax.numpy as jnp
from jax import lax
from jax.experimental import pallas as pl
from jax.experimental.pallas import tpu as pltpu
from jax.sharding import PartitionSpec as P

MESH = pl.DeviceIdType.MESH
F32 = jnp.float32
BF16 = jnp.bfloat16
T = 128
NCHUNK = 4
SLOTS = 84
GROUP = 32
UNROLL = 6
HALF = SLOTS // 2
SEMS = 200


def wrap4(value):
    return lax.rem(value, 4)


class Ring:
    def __init__(self, k, src, unit, rl, rr, fl, fr, out, right, left):
        self.src, self.unit, self.out = src, unit, out
        self.rl, self.rr, self.fl, self.fr = rl, rr, fl, fr
        u = unit
        self.to_right = k.copy(src.at[pl.ds(3 * u, 2 * u)], rl, right)
        self.to_left = k.copy(src.at[pl.ds(5 * u, 2 * u)], rr, left)
        self.sum_right = k.copy(src.at[pl.ds(2 * u, u)], fl, right)
        self.sum_left = k.copy(src.at[pl.ds(7 * u, u)], fr, left)

    def first(self):
        self.to_right.start()
        self.to_left.start()

    def second(self):
        u, src = self.unit, self.src
        self.to_right.wait_recv()
        src[pl.ds(2 * u, u)] = (
            src[pl.ds(2 * u, u)].astype(F32) + self.rl[pl.ds(u, u)].astype(F32)
        ).astype(BF16)
        self.sum_right.start()
        self.to_left.wait_recv()
        src[pl.ds(7 * u, u)] = (
            src[pl.ds(7 * u, u)].astype(F32) + self.rr[pl.ds(0, u)].astype(F32)
        ).astype(BF16)
        self.sum_left.start()

    def last(self):
        u, src = self.unit, self.src
        self.sum_right.wait_recv()
        self.out[pl.ds(0, u)] = (
            src[pl.ds(0, u)].astype(F32)
            + self.fl[...].astype(F32)
            + self.rr[pl.ds(u, u)].astype(F32)
        ).astype(BF16)
        self.sum_left.wait_recv()
        self.out[pl.ds(u, u)] = (
            src[pl.ds(u, u)].astype(F32)
            + self.rl[pl.ds(0, u)].astype(F32)
            + self.fr[...].astype(F32)
        ).astype(BF16)


class Fan:
    def __init__(self, k, src, unit, landed, devices):
        self.src, self.unit, self.landed = src, unit, landed
        self.sends = [
            k.copy(src.at[pl.ds(s * unit, unit)], landed.at[pl.ds((s - 1) * unit, unit)], devices[s - 1])
            for s in (1, 2, 3)
        ]

    def first(self):
        for s in (1, 0, 2):
            self.sends[s].start()

    def arrived(self):
        for sent in self.sends:
            sent.wait_recv()


class Copies:
    def __init__(self, send_sems, recv_sems):
        self.send_sems, self.recv_sems, self.used = send_sems, recv_sems, 0
        self.all = []

    def copy(self, src, dst, device):
        index = self.used
        self.used += 1
        made = pltpu.make_async_remote_copy(
            src_ref=src,
            dst_ref=dst,
            send_sem=self.send_sems.at[index],
            recv_sem=self.recv_sems.at[index],
            device_id=device,
            device_id_type=MESH,
        )
        self.all.append(made)
        return made

    def swap(self, src, dst, device):
        sent = self.copy(src, src, device)
        came = pltpu.make_async_remote_copy(
            src_ref=dst,
            dst_ref=dst,
            send_sem=self.send_sems.at[self.used - 1],
            recv_sem=self.recv_sems.at[self.used - 1],
            device_id=device,
            device_id_type=MESH,
        )
        return sent, came


def kernel(
    count_ref, rows_ref, cols_ref, grad_hbm, mask_hbm, agg_hbm, weight_hbm, tiles_hbm,
    node_ref, wgrad_ref,
    grad_v, mask_v, agg_v, weight_v,
    tiles, seg, acc_ref,
    g0, g1, g2, g3,
    parts, xl, xr, xfl, xfr, mids, landed, tops, ztop,
    wl, ws, wa, wxl, wxr, wxfl, wxfr, wb, wyl, wyr, wyfl, wyfr, wc, wq, wn, wg,
    lists, places, gates, place_s, gate_s,
    send_sems, recv_sems, line_send, line_recv, share_send, share_recv, local_sems,
):
    row, col, depth = lax.axis_index("row"), lax.axis_index("col"), lax.axis_index("depth")
    x, y = lax.div(row, 4), lax.rem(row, 4)
    z, core = lax.div(col, 2), lax.rem(col, 2)
    zz = depth * 8 + z
    quad = lax.rem(z, 4)
    quads = lax.div(zz, 4)
    gathered = (g0, g1, g2, g3)

    def device(dx=0, dy=0):
        return (wrap4(x + dx) * 4 + wrap4(y + dy), col, depth)

    def along_z(step):
        place = lax.rem(zz + step, 16)
        return (row, lax.rem(place, 8) * 2 + core, lax.div(place, 8))

    def in_quad(step):
        return (row, (z - quad + wrap4(quad + step)) * 2 + core, depth)

    sibling = (row, z * 2 + 1 - core, depth)
    right_x, left_x = device(dx=1), device(dx=3)
    right_y, left_y = device(dy=1), device(dy=3)
    all_x = [device(dx=s) for s in (1, 2, 3)]
    all_y = [device(dy=s) for s in (1, 2, 3)]
    partner = (row, col, 1 - depth)
    k = Copies(send_sems, recv_sems)

    loads = [
        pltpu.make_async_copy(src, dst, local_sems.at[i])
        for i, (src, dst) in enumerate((
            (grad_hbm, grad_v), (mask_hbm, mask_v), (weight_hbm, weight_v), (agg_hbm, agg_v), (tiles_hbm, tiles),
        ))
    ]
    for load in loads:
        load.start()

    barrier = pltpu.get_barrier_semaphore()
    peers = [sibling] + all_x + all_y + [along_z(s) for s in (1, 15, 2, 14, 4, 8, 12)]
    peers += [in_quad(s) for s in (1, 2, 3)]
    for peer in peers:
        pl.semaphore_signal(barrier, inc=1, device_id=peer, device_id_type=MESH)

    for load in loads[:3]:
        load.wait()
    grad_v[...] = grad_v[...] * mask_v[...].astype(F32).astype(BF16)
    own = core * 8 + z
    for c in range(NCHUNK):
        gathered[c][own] = lax.dot_general(
            weight_v[pl.ds(c * T, T), :], grad_v[...], (((1,), (1,)), ((), ())),
            preferred_element_type=F32,
        ).astype(BF16)
    pl.semaphore_wait(barrier, len(peers))

    def there(place):
        return (place >= 0) & (place <= 7)

    def line(c, source, sign, hop, device=None):
        block = gathered[c].at[core * 8 + source]
        return pltpu.make_async_remote_copy(
            src_ref=block, dst_ref=block,
            send_sem=line_send.at[c, source, hop + (1 if sign > 0 else -1)],
            recv_sem=line_recv.at[c, source],
            device_id=device or (row, (z + sign * hop) * 2 + core, depth), device_id_type=MESH,
        )

    def share(c, source, side):
        block = gathered[c].at[side * 8 + source]
        return pltpu.make_async_remote_copy(
            src_ref=block, dst_ref=block,
            send_sem=share_send.at[c, source], recv_sem=share_recv.at[c, source],
            device_id=sibling, device_id_type=MESH,
        )

    def each_send(c, source, sign, act):
        for hop in (2, 1):
            @pl.when(there(z + sign * hop))
            def _():
                act(line(c, source, sign, hop))

    def begin(c):
        for sign in (1, -1):
            each_send(c, z, sign, lambda made: made.start())
        share(c, z, core).start()

    def forward(c, m):
        for sign in (1, -1):
            source = z - sign * 2 * m

            @pl.when(there(source))
            def _():
                line(c, source, sign, 1, sibling).wait_recv()
                each_send(c, source, sign, lambda made: made.start())
                share(c, source, core).start()

    def deliver(c):
        for m in range(4):
            for sign in (1, -1):
                source = z - sign * (2 * m + 1)

                @pl.when(there(source))
                def _():
                    line(c, source, sign, 1, sibling).wait_recv()
                    share(c, source, core).start()

    def shared(c):
        for source in range(8):
            share(c, source, 1 - core).wait_recv()

    def line_end():
        for c in range(NCHUNK):
            for m in range(4):
                for sign in (1, -1):
                    source = z - sign * 2 * m

                    @pl.when(there(source))
                    def _():
                        each_send(c, source, sign, lambda made: made.wait_send())
            for source in range(8):
                share(c, source, core).wait_send()

    w_share = k.copy(wl.at[1 - core], ws, sibling)
    w_x = Ring(k, wa, 128, wxl, wxr, wxfl, wxfr, wb, right_x, left_x)
    w_y = Ring(k, wb, 32, wyl, wyr, wyfl, wyfr, wc, right_y, left_y)
    w_q = [
        k.copy(wc.at[pl.ds(pl.multiple_of(wrap4(quad + s) * 16, 16), 16)], wq.at[s - 1], in_quad(s))
        for s in (1, 2, 3)
    ]
    w_n = [
        k.swap(wn.at[quads], wn.at[wrap4(quads + 4 - s)], along_z(4 * s)) for s in (1, 2, 3)
    ]

    def strip(place):
        return wg.at[core, x, y, pl.ds(pl.multiple_of(place * 16, 16), 16)]

    w_back_q = [k.swap(strip(quad), strip(wrap4(quad + 4 - s)), in_quad(s)) for s in (1, 2, 3)]
    w_back_y = [
        k.swap(wg.at[core, x, y], wg.at[core, x, wrap4(y + 4 - s)], device(dy=s)) for s in (1, 2, 3)
    ]
    w_back_x = [
        k.swap(wg.at[core, x], wg.at[core, wrap4(x + 4 - s)], device(dx=s)) for s in (1, 2, 3)
    ]
    w_back_core = k.swap(wg.at[core], wg.at[1 - core], sibling)

    def weight_0():
        loads[3].wait()
        for h in range(2):
            for q in range(4):
                wl[h, q] = lax.dot_general(
                    agg_v[:, h * 256:(h + 1) * 256], grad_v[:, q * T:(q + 1) * T],
                    (((0,), (0,)), ((), ())), preferred_element_type=F32,
                ).astype(BF16)
        w_share.start()

    def weight_1():
        w_share.wait_recv()
        for a in range(4):
            xt = wrap4(x + a)
            for b in range(4):
                rows = pl.ds(pl.multiple_of(wrap4(y + b) * 64, 64), 64)
                wa[pl.ds(a * 256 + b * 64, 64)] = (
                    wl[core, xt, rows].astype(F32) + ws[xt, rows].astype(F32)
                ).astype(BF16)
        w_x.first()

    def weight_2():
        w_x.second()

    def weight_3():
        w_x.last()
        w_y.first()

    def weight_4():
        w_y.second()

    def weight_5():
        w_y.last()
        for sent in w_q:
            sent.start()

    def weight_6():
        total = wc[pl.ds(pl.multiple_of(quad * 16, 16), 16)].astype(F32)
        for s in range(3):
            w_q[s].wait_recv()
            total = total + wq[s].astype(F32)
        wn[quads] = total.astype(BF16)
        for sent, _ in w_n:
            sent.start()

    def weight_7():
        for _, came in w_n:
            came.wait_recv()
        total = wn[0].astype(F32)
        for place in range(1, 4):
            total = total + wn[place].astype(F32)
        wg[core, x, y, pl.ds(pl.multiple_of(quad * 16, 16), 16)] = total.astype(BF16)
        for sent, _ in w_back_q:
            sent.start()

    def weight_8():
        for _, came in w_back_q:
            came.wait_recv()
        for sent, _ in w_back_y:
            sent.start()

    def weight_9():
        for _, came in w_back_y:
            came.wait_recv()
        for sent, _ in w_back_x:
            sent.start()

    def weight_10():
        for _, came in w_back_x:
            came.wait_recv()
        w_back_core[0].start()

    def weight_11():
        w_back_core[1].wait_recv()
        for h in range(2):
            for a in range(4):
                for b in range(4):
                    wgrad_ref[pl.ds(h * 256 + b * 64, 64), a * T:(a + 1) * T] = wg[h, a, b]

    def sort():
        lane = lax.broadcasted_iota(jnp.int32, (1, T), 1)
        lists[...] = jnp.zeros((8, T), jnp.int32)
        lists[0:1, 0:SLOTS] = cols_ref[...]
        lists[1:2, 0:SLOTS] = rows_ref[...]
        key = jnp.where(lane < count_ref[0], lists[0:1, :], GROUP)
        key = jnp.where(lane < SLOTS, key, GROUP)
        tile_row = lists[1:2, :]
        slab_place = (tile_row & 1) * 8 + (tile_row >> 1)
        above = lax.broadcasted_iota(jnp.int32, (T, T), 0)
        across = lax.broadcasted_iota(jnp.int32, (T, T), 1)

        def wide(value):
            return jnp.broadcast_to(value, (T, T))

        def count(mask, value=1):
            return jnp.sum(jnp.where(mask, value, 0), axis=0, keepdims=True)

        key_a = wide(key)
        key_t = key_a.T
        same = (key_t == key_a) & (above < across)
        rank = count((key_t < key_a) | same)
        follows = jnp.minimum(count(same), 1)
        chosen = wide(rank).T == across
        places[0:1, :] = jnp.minimum(count(chosen, above), SLOTS - 1)
        places[1:2, :] = jnp.minimum(count(chosen, wide(slab_place).T), 15)
        places[2:3, :] = jnp.clip(count(key_t <= across) - 1, 0, SLOTS - 1)
        gates[0:1, :] = count(chosen, wide(follows).T).astype(F32)
        gates[1:2, :] = jnp.minimum(count(key_t == across), 1).astype(F32)
        for made in (
            pltpu.make_async_copy(places, place_s, local_sems.at[5]),
            pltpu.make_async_copy(gates, gate_s, local_sems.at[6]),
        ):
            made.start()
            made.wait()

    def compute(c, first, stop):
        def block(step, acc):
            for inner in range(UNROLL):
                p = first + step * UNROLL + inner
                product = jnp.dot(
                    gathered[c][place_s[1, p]], tiles[place_s[0, p]],
                    preferred_element_type=F32,
                )
                acc = acc * gate_s[0, p] + product
                seg[p] = acc.astype(BF16)
            return acc

        if first == 0:
            start = jnp.zeros((T, T), F32)
        else:
            start = acc_ref[...]
        end = lax.fori_loop(0, (stop - first) // UNROLL, block, start)
        if stop < SLOTS:
            acc_ref[...] = end

    def place(c):
        def one(m, carry):
            major, minor = lax.div(m, 4), lax.rem(m, 4)
            rows = pl.ds(pl.multiple_of(m * T, T), T)
            for dt in range(2):
                a, b = (major, minor) if dt == 0 else (minor, major)
                target = (wrap4(x + a) * 4 + wrap4(y + b)) * 2 + dt
                parts[c, dt, rows] = (
                    seg[place_s[2, target]].astype(F32) * gate_s[1, target]
                ).astype(BF16)
            return carry

        lax.fori_loop(0, 16, one, 0)

    ring, fan, cross = [], [], []
    for c in range(NCHUNK):
        for dt in range(2):
            far = (right_x, left_x) if dt == 0 else (right_y, left_y)
            ring.append(Ring(
                k, parts.at[c, dt], 256, xl.at[c, dt], xr.at[c, dt], xfl.at[c, dt], xfr.at[c, dt],
                mids.at[c, dt], *far,
            ))
            fan.append(Fan(k, mids.at[c, dt], T, landed.at[c, dt], all_y if dt == 0 else all_x))
        cross.append(k.copy(tops.at[c, 1 - depth], ztop.at[c], partner))

    def reduce_1(c):
        for dt in range(2):
            ring[2 * c + dt].first()

    def reduce_2(c):
        for dt in range(2):
            ring[2 * c + dt].second()

    def reduce_3(c):
        for dt in range(2):
            ring[2 * c + dt].last()
            fan[2 * c + dt].first()

    def reduce_4(c):
        for dt in range(2):
            fan[2 * c + dt].arrived()
        for turn, dt in enumerate((1 - depth, depth)):
            total = mids[c, dt, 0:T].astype(F32)
            for s in range(3):
                total = total + landed[c, dt, s * T:(s + 1) * T].astype(F32)
            tops[c, dt] = total.astype(BF16)
            if turn == 0:
                cross[c].start()

    def reduce_5(c):
        cross[c].wait_recv()
        node_ref[pl.ds(c * T, T)] = (
            tops[c, depth].astype(F32) + ztop[c].astype(F32)
        ).astype(BF16)

    begin(0)
    begin(1)
    sort()
    weight_0()
    forward(0, 1)
    begin(2)
    forward(1, 1)
    weight_1()
    forward(0, 2)
    forward(1, 2)
    begin(3)
    forward(2, 1)
    weight_2()
    forward(0, 3)
    deliver(0)
    forward(1, 3)
    forward(2, 2)
    forward(3, 1)
    loads[4].wait()
    shared(0)

    compute(0, 0, HALF)
    weight_3()
    forward(2, 3)
    forward(3, 2)
    compute(0, HALF, SLOTS)
    place(0)
    reduce_1(0)
    deliver(1)
    forward(3, 3)
    shared(1)

    compute(1, 0, HALF)
    reduce_2(0)
    weight_4()
    compute(1, HALF, SLOTS)
    place(1)
    reduce_1(1)
    deliver(2)
    reduce_3(0)
    shared(2)

    compute(2, 0, HALF)
    reduce_2(1)
    weight_5()
    reduce_4(0)
    compute(2, HALF, SLOTS)
    place(2)
    reduce_1(2)
    deliver(3)
    reduce_3(1)
    weight_6()
    shared(3)

    compute(3, 0, HALF)
    reduce_2(2)
    weight_7()
    reduce_4(1)
    compute(3, HALF, SLOTS)
    place(3)
    reduce_1(3)

    weight_8()
    reduce_3(2)
    reduce_5(0)
    weight_9()
    reduce_2(3)
    reduce_4(2)
    weight_10()
    reduce_3(3)
    reduce_5(1)
    weight_11()
    reduce_4(3)
    reduce_5(2)
    reduce_5(3)
    for made in k.all:
        made.wait_send()
    line_end()


def on_device(
    grad_out, relu_mask, aggregated, weight, adjacency_tiles, tile_rows, tile_cols, tile_count
):
    smem = pl.BlockSpec(memory_space=pltpu.SMEM)
    vmem = pl.BlockSpec(memory_space=pltpu.VMEM)
    hbm = pl.BlockSpec(memory_space=pltpu.HBM)
    bf = lambda *shape: pltpu.VMEM(shape, BF16)
    node_t, wgrad = pl.pallas_call(
        kernel,
        out_shape=(
            jax.ShapeDtypeStruct((NCHUNK * T, T), BF16),
            jax.ShapeDtypeStruct((512, 512), BF16),
        ),
        in_specs=[smem, vmem, vmem, hbm, hbm, hbm, hbm, hbm],
        out_specs=(vmem, vmem),
        scratch_shapes=[
            bf(T, 512), pltpu.VMEM((T, 512), jnp.int32), bf(T, 512), bf(512, 512),
            bf(SLOTS, T, T), bf(SLOTS, T, T), pltpu.VMEM((T, T), F32),
            bf(16, T, T), bf(16, T, T), bf(16, T, T), bf(16, T, T),
            bf(4, 2, 16 * T, T),
            bf(4, 2, 512, T), bf(4, 2, 512, T), bf(4, 2, 256, T), bf(4, 2, 256, T),
            bf(4, 2, 512, T),
            bf(4, 2, 3 * T, T),
            bf(4, 2, T, T), bf(4, T, T),
            bf(2, 4, 256, T), bf(4, 256, T), bf(1024, T),
            bf(256, T), bf(256, T), bf(128, T), bf(128, T),
            bf(256, T),
            bf(64, T), bf(64, T), bf(32, T), bf(32, T),
            bf(64, T), bf(3, 16, T), bf(4, 16, T), bf(2, 4, 4, 64, T),
            pltpu.VMEM((8, T), jnp.int32), pltpu.VMEM((8, T), jnp.int32), pltpu.VMEM((8, T), F32),
            pltpu.SMEM((8, T), jnp.int32), pltpu.SMEM((8, T), F32),
            pltpu.SemaphoreType.DMA((SEMS,)),
            pltpu.SemaphoreType.DMA((SEMS,)),
            pltpu.SemaphoreType.DMA((4, 8, 4)),
            pltpu.SemaphoreType.DMA((4, 8)),
            pltpu.SemaphoreType.DMA((4, 8)),
            pltpu.SemaphoreType.DMA((4, 8)),
            pltpu.SemaphoreType.DMA((7,)),
        ],
        compiler_params=pltpu.CompilerParams(
            collective_id=0, has_side_effects=True, vmem_limit_bytes=60 * 1024 * 1024
        ),
        cost_estimate=pl.CostEstimate(flops=1_600_000_000, bytes_accessed=5_000_000, transcendentals=0),
    )(
        tile_count, tile_rows.reshape(1, SLOTS), tile_cols.reshape(1, SLOTS),
        grad_out, relu_mask, aggregated, weight, adjacency_tiles,
    )
    return (node_t.T, wgrad.astype(F32))


def solution(mesh):
    return jax.shard_map(
        on_device,
        mesh=mesh,
        in_specs=(
            P(("row", "col", "depth"), None),
            P(("row", "col", "depth"), None),
            P(("row", "col", "depth"), None),
            P(),
            P(("row", "col", "depth"), None, None),
            P(("row", "col", "depth")),
            P(("row", "col", "depth")),
            P(("row", "col", "depth")),
        ),
        out_specs=(P(("row", "col", "depth"), None), P()),
        check_vma=False,
    )
```

```python
import jax
import jax.numpy as jnp
from jax import lax
from jax.experimental import pallas as pl
from jax.experimental.pallas import tpu as pltpu
from jax.sharding import PartitionSpec as P

MESH = pl.DeviceIdType.MESH
F32 = jnp.float32
BF16 = jnp.bfloat16
T = 128
CHUNKS = (128, 128, 128, 128)
NCHUNK = len(CHUNKS)
STARTS = tuple(sum(CHUNKS[:c]) for c in range(NCHUNK))
SLOTS = 84
GROUP = 32
UNROLL = 6
HALF = SLOTS // 2
SEMS = 112


def wrap4(value):
    return lax.rem(value, 4)


class Ring:
    def __init__(self, k, src, unit, rl, rr, fl, fr, out, right, left):
        self.src, self.unit, self.out = src, unit, out
        self.rl, self.rr, self.fl, self.fr = rl, rr, fl, fr
        u = unit
        self.to_right = k.copy(src.at[pl.ds(3 * u, 2 * u)], rl, right)
        self.to_left = k.copy(src.at[pl.ds(5 * u, 2 * u)], rr, left)
        self.sum_right = k.copy(src.at[pl.ds(2 * u, u)], fl, right)
        self.sum_left = k.copy(src.at[pl.ds(7 * u, u)], fr, left)

    def first(self):
        self.to_right.start()
        self.to_left.start()

    def settle(self):
        for sent in (self.to_right, self.to_left, self.sum_right, self.sum_left):
            sent.wait_send()

    def second(self):
        u, src = self.unit, self.src
        self.to_right.wait_recv()
        src[pl.ds(2 * u, u)] = (
            src[pl.ds(2 * u, u)].astype(F32) + self.rl[pl.ds(u, u)].astype(F32)
        ).astype(BF16)
        self.sum_right.start()
        self.to_left.wait_recv()
        src[pl.ds(7 * u, u)] = (
            src[pl.ds(7 * u, u)].astype(F32) + self.rr[pl.ds(0, u)].astype(F32)
        ).astype(BF16)
        self.sum_left.start()

    def last(self):
        u, src = self.unit, self.src
        self.sum_right.wait_recv()
        self.out[pl.ds(0, u)] = (
            src[pl.ds(0, u)].astype(F32)
            + self.fl[...].astype(F32)
            + self.rr[pl.ds(u, u)].astype(F32)
        ).astype(BF16)
        self.sum_left.wait_recv()
        self.out[pl.ds(u, u)] = (
            src[pl.ds(u, u)].astype(F32)
            + self.rl[pl.ds(0, u)].astype(F32)
            + self.fr[...].astype(F32)
        ).astype(BF16)


class Fan:
    def __init__(self, k, src, unit, landed, devices):
        self.src, self.unit, self.landed = src, unit, landed
        self.sends = [
            k.copy(src.at[pl.ds(s * unit, unit)], landed.at[pl.ds((s - 1) * unit, unit)], devices[s - 1])
            for s in (1, 2, 3)
        ]

    def first(self):
        for s in (1, 0, 2):
            self.sends[s].start()

    def settle(self):
        for sent in self.sends:
            sent.wait_send()

    def arrived(self):
        for sent in self.sends:
            sent.wait_recv()

    def total(self):
        u = self.unit
        value = self.src[pl.ds(0, u)].astype(F32)
        for s in range(3):
            value = value + self.landed[pl.ds(s * u, u)].astype(F32)
        return value


class Copies:
    def __init__(self, send_sems, recv_sems):
        self.send_sems, self.recv_sems, self.used = send_sems, recv_sems, 0

    def copy(self, src, dst, device):
        index = self.used
        self.used += 1
        made = pltpu.make_async_remote_copy(
            src_ref=src,
            dst_ref=dst,
            send_sem=self.send_sems.at[index],
            recv_sem=self.recv_sems.at[index],
            device_id=device,
            device_id_type=MESH,
        )
        return made

    def swap(self, src, dst, device):
        sent = self.copy(src, src, device)
        came = pltpu.make_async_remote_copy(
            src_ref=dst,
            dst_ref=dst,
            send_sem=self.send_sems.at[self.used - 1],
            recv_sem=self.recv_sems.at[self.used - 1],
            device_id=device,
            device_id_type=MESH,
        )
        return sent, came


def kernel(
    count_ref, rows_ref, cols_ref, grad_hbm, mask_hbm, agg_hbm, weight_hbm, tiles_hbm,
    node_ref, wgrad_ref,
    grad_v, mask_v, agg_v, weight_v,
    tiles, seg, acc_ref,
    gathered, parts, xl, xr, xfl, xfr, mids, landed, tops, ztop,
    wl, ws, wa, wxd, wb, wyd, wc, wq, wn, wg,
    lists, places, gates, place_s, gate_s,
    send_sems, recv_sems, line_send, line_recv, share_send, share_recv, local_sems,
):
    row, col, depth = lax.axis_index("row"), lax.axis_index("col"), lax.axis_index("depth")
    x, y = lax.div(row, 4), lax.rem(row, 4)
    z, core = lax.div(col, 2), lax.rem(col, 2)
    zz = depth * 8 + z
    quad = lax.rem(z, 4)
    quads = lax.div(zz, 4)

    def device(dx=0, dy=0):
        return (wrap4(x + dx) * 4 + wrap4(y + dy), col, depth)

    def along_z(step):
        place = lax.rem(zz + step, 16)
        return (row, lax.rem(place, 8) * 2 + core, lax.div(place, 8))

    def in_quad(step):
        return (row, (z - quad + wrap4(quad + step)) * 2 + core, depth)

    sibling = (row, z * 2 + 1 - core, depth)
    right_x, left_x = device(dx=1), device(dx=3)
    right_y, left_y = device(dy=1), device(dy=3)
    all_x = [device(dx=s) for s in (1, 2, 3)]
    all_y = [device(dy=s) for s in (1, 2, 3)]
    partner = (row, col, 1 - depth)
    k = Copies(send_sems, recv_sems)

    loads = [
        pltpu.make_async_copy(src, dst, local_sems.at[i])
        for i, (src, dst) in enumerate((
            (grad_hbm, grad_v), (mask_hbm, mask_v), (weight_hbm, weight_v), (agg_hbm, agg_v), (tiles_hbm, tiles),
        ))
    ]
    for load in loads:
        load.start()

    barrier = pltpu.get_barrier_semaphore()
    peers = [sibling] + all_x + all_y + [along_z(s) for s in (1, 15, 2, 14, 4, 8, 12)]
    peers += [in_quad(s) for s in (1, 2, 3)]
    for peer in peers:
        pl.semaphore_signal(barrier, inc=1, device_id=peer, device_id_type=MESH)

    for load in loads[:3]:
        load.wait()
    grad_v[...] = grad_v[...] * mask_v[...].astype(F32).astype(BF16)
    own = core * 8 + z
    for c in range(NCHUNK):
        gathered[c][own] = lax.dot_general(
            weight_v[pl.ds(STARTS[c], CHUNKS[c]), :], grad_v[...], (((1,), (1,)), ((), ())),
            preferred_element_type=F32,
        ).astype(BF16)
    pl.semaphore_wait(barrier, len(peers))

    def there(place):
        return (place >= 0) & (place <= 7)

    def line(c, source, sign, hop, device=None):
        block = gathered[c].at[core * 8 + source]
        return pltpu.make_async_remote_copy(
            src_ref=block, dst_ref=block,
            send_sem=line_send.at[c, source, hop + (1 if sign > 0 else -1)],
            recv_sem=line_recv.at[c, source],
            device_id=device or (row, (z + sign * hop) * 2 + core, depth), device_id_type=MESH,
        )

    def share(c, side):
        half = gathered[c].at[pl.ds(side * 8, 8)]
        return pltpu.make_async_remote_copy(
            src_ref=half, dst_ref=half,
            send_sem=share_send.at[c], recv_sem=share_recv.at[c],
            device_id=sibling, device_id_type=MESH,
        )

    def each_send(c, source, sign, act):
        for hop in (2, 1):
            @pl.when(there(z + sign * hop))
            def _():
                act(line(c, source, sign, hop))

    def begin(c):
        for sign in (1, -1):
            each_send(c, z, sign, lambda made: made.start())

    def forward(c, m):
        for sign in (1, -1):
            source = z - sign * 2 * m

            @pl.when(there(source))
            def _():
                line(c, source, sign, 1, sibling).wait_recv()
                each_send(c, source, sign, lambda made: made.start())

    def deliver(c):
        for m in range(4):
            for sign in (1, -1):
                source = z - sign * (2 * m + 1)

                @pl.when(there(source))
                def _():
                    line(c, source, sign, 1, sibling).wait_recv()
        share(c, core).start()

    def shared(c):
        share(c, 1 - core).wait_recv()

    def line_end(c):
        for m in range(4):
            for sign in (1, -1):
                source = z - sign * 2 * m

                @pl.when(there(source))
                def _():
                    each_send(c, source, sign, lambda made: made.wait_send())
        share(c, core).wait_send()

    w_share = k.copy(wl.at[1 - core], ws, sibling)
    w_x = Fan(k, wa, 256, wxd, all_x)
    w_y = Fan(k, wb, 64, wyd, all_y)
    w_q = [
        k.copy(wc.at[pl.ds(pl.multiple_of(wrap4(quad + s) * 16, 16), 16)], wq.at[s - 1], in_quad(s))
        for s in (1, 2, 3)
    ]
    w_n = [
        k.swap(wn.at[quads], wn.at[wrap4(quads + 4 - s)], along_z(4 * s)) for s in (1, 2, 3)
    ]

    def strip(place):
        return wg.at[core, x, y, pl.ds(pl.multiple_of(place * 16, 16), 16)]

    w_back_q = [k.swap(strip(quad), strip(wrap4(quad + 4 - s)), in_quad(s)) for s in (1, 2, 3)]
    w_back_y = [
        k.swap(wg.at[core, x, y], wg.at[core, x, wrap4(y + 4 - s)], device(dy=s)) for s in (1, 2, 3)
    ]
    w_back_x = [
        k.swap(wg.at[core, x], wg.at[core, wrap4(x + 4 - s)], device(dx=s)) for s in (1, 2, 3)
    ]
    w_back_core = k.swap(wg.at[core], wg.at[1 - core], sibling)

    def weight_0():
        loads[3].wait()
        for h in range(2):
            for q in range(4):
                wl[h, q] = lax.dot_general(
                    agg_v[:, h * 256:(h + 1) * 256], grad_v[:, q * T:(q + 1) * T],
                    (((0,), (0,)), ((), ())), preferred_element_type=F32,
                ).astype(BF16)
        w_share.start()

    def weight_1():
        w_share.wait_recv()
        for a in range(4):
            xt = wrap4(x + a)
            for b in range(4):
                rows = pl.ds(pl.multiple_of(wrap4(y + b) * 64, 64), 64)
                wa[pl.ds(a * 256 + b * 64, 64)] = (
                    wl[core, xt, rows].astype(F32) + ws[xt, rows].astype(F32)
                ).astype(BF16)
        w_x.first()
        w_share.wait_send()

    def weight_2():
        w_x.arrived()
        wb[...] = w_x.total().astype(BF16)
        w_y.first()
        w_x.settle()

    def weight_3():
        w_y.arrived()
        wc[...] = w_y.total().astype(BF16)
        for sent in w_q:
            sent.start()
        w_y.settle()

    def weight_4():
        total = wc[pl.ds(pl.multiple_of(quad * 16, 16), 16)].astype(F32)
        for s in range(3):
            w_q[s].wait_recv()
            total = total + wq[s].astype(F32)
        wn[quads] = total.astype(BF16)
        for sent, _ in w_n:
            sent.start()
        for sent in w_q:
            sent.wait_send()

    def weight_5():
        for _, came in w_n:
            came.wait_recv()
        total = wn[0].astype(F32)
        for place in range(1, 4):
            total = total + wn[place].astype(F32)
        wg[core, x, y, pl.ds(pl.multiple_of(quad * 16, 16), 16)] = total.astype(BF16)
        for sent, _ in w_back_q:
            sent.start()
        for sent, _ in w_n:
            sent.wait_send()

    def weight_6():
        for _, came in w_back_q:
            came.wait_recv()
        for sent, _ in w_back_y:
            sent.start()
        for sent, _ in w_back_q:
            sent.wait_send()

    def weight_7():
        for _, came in w_back_y:
            came.wait_recv()
        for sent, _ in w_back_x:
            sent.start()
        for sent, _ in w_back_y:
            sent.wait_send()

    def weight_8():
        for _, came in w_back_x:
            came.wait_recv()
        w_back_core[0].start()
        for sent, _ in w_back_x:
            sent.wait_send()

    def weight_9():
        w_back_core[1].wait_recv()
        w_back_core[0].wait_send()
        for h in range(2):
            for a in range(4):
                for b in range(4):
                    wgrad_ref[pl.ds(h * 256 + b * 64, 64), a * T:(a + 1) * T] = wg[h, a, b]

    def sort():
        lane = lax.broadcasted_iota(jnp.int32, (1, T), 1)
        lists[...] = jnp.zeros((8, T), jnp.int32)
        lists[0:1, 0:SLOTS] = cols_ref[...]
        lists[1:2, 0:SLOTS] = rows_ref[...]
        key = jnp.where(lane < count_ref[0], lists[0:1, :], GROUP)
        key = jnp.where(lane < SLOTS, key, GROUP)
        tile_row = lists[1:2, :]
        slab_place = (tile_row & 1) * 8 + (tile_row >> 1)
        above = lax.broadcasted_iota(jnp.int32, (T, T), 0)
        across = lax.broadcasted_iota(jnp.int32, (T, T), 1)

        def wide(value):
            return jnp.broadcast_to(value, (T, T))

        def count(mask, value=1):
            return jnp.sum(jnp.where(mask, value, 0), axis=0, keepdims=True)

        key_a = wide(key)
        key_t = key_a.T
        same = (key_t == key_a) & (above < across)
        rank = count((key_t < key_a) | same)
        follows = jnp.minimum(count(same), 1)
        chosen = wide(rank).T == across
        places[0:1, :] = jnp.minimum(count(chosen, above), SLOTS - 1)
        places[1:2, :] = jnp.minimum(count(chosen, wide(slab_place).T), 15)
        places[2:3, :] = jnp.clip(count(key_t <= across) - 1, 0, SLOTS - 1)
        gates[0:1, :] = count(chosen, wide(follows).T).astype(F32)
        gates[1:2, :] = jnp.minimum(count(key_t == across), 1).astype(F32)
        for made in (
            pltpu.make_async_copy(places, place_s, local_sems.at[5]),
            pltpu.make_async_copy(gates, gate_s, local_sems.at[6]),
        ):
            made.start()
            made.wait()

    def compute(c, first, stop):
        width = CHUNKS[c]

        def block(step, acc):
            for inner in range(UNROLL):
                p = first + step * UNROLL + inner
                product = jnp.dot(
                    gathered[c][place_s[1, p]], tiles[place_s[0, p]],
                    preferred_element_type=F32,
                )
                acc = acc * gate_s[0, p] + product
                seg[p, 0:width] = acc.astype(BF16)
            return acc

        if first == 0:
            start = jnp.zeros((width, T), F32)
        else:
            start = acc_ref[0:width]
        end = lax.fori_loop(0, (stop - first) // UNROLL, block, start)
        if stop < SLOTS:
            acc_ref[0:width] = end

    def place(c):
        width = CHUNKS[c]

        def one(m, carry):
            major, minor = lax.div(m, 4), lax.rem(m, 4)
            rows = pl.ds(pl.multiple_of(m * width, width), width)
            for dt in range(2):
                a, b = (major, minor) if dt == 0 else (minor, major)
                target = (wrap4(x + a) * 4 + wrap4(y + b)) * 2 + dt
                parts[c][dt, rows] = (
                    seg[place_s[2, target], 0:width].astype(F32) * gate_s[1, target]
                ).astype(BF16)
            return carry

        lax.fori_loop(0, 16, one, 0)

    ring, fan, cross = [], [], []
    for c in range(NCHUNK):
        for dt in range(2):
            far = (right_x, left_x) if dt == 0 else (right_y, left_y)
            ring.append(Ring(
                k, parts[c].at[dt], 2 * CHUNKS[c],
                xl[c].at[dt], xr[c].at[dt], xfl[c].at[dt], xfr[c].at[dt], mids[c].at[dt], *far,
            ))
            fan.append(Fan(
                k, mids[c].at[dt], CHUNKS[c], landed[c].at[dt], all_y if dt == 0 else all_x
            ))
        cross.append(k.copy(tops[c].at[1 - depth], ztop[c], partner))

    def reduce_1(c):
        for dt in range(2):
            ring[2 * c + dt].first()

    def reduce_2(c):
        for dt in range(2):
            ring[2 * c + dt].second()

    def reduce_3(c):
        for dt in range(2):
            ring[2 * c + dt].last()
            fan[2 * c + dt].first()
        for dt in range(2):
            ring[2 * c + dt].settle()

    def reduce_4(c):
        for dt in range(2):
            fan[2 * c + dt].arrived()
        width = CHUNKS[c]
        for turn, dt in enumerate((1 - depth, depth)):
            total = mids[c][dt, 0:width].astype(F32)
            for s in range(3):
                total = total + landed[c][dt, s * width:(s + 1) * width].astype(F32)
            tops[c][dt] = total.astype(BF16)
            if turn == 0:
                cross[c].start()
        for dt in range(2):
            fan[2 * c + dt].settle()

    def reduce_5(c):
        cross[c].wait_send()
        cross[c].wait_recv()
        node_ref[pl.ds(STARTS[c], CHUNKS[c])] = (
            tops[c][depth].astype(F32) + ztop[c][...].astype(F32)
        ).astype(BF16)

    begin(0)
    sort()
    begin(1)
    begin(2)
    weight_0()
    forward(0, 1)
    weight_1()
    forward(1, 1)
    forward(2, 1)
    forward(0, 2)
    forward(1, 2)
    begin(3)
    weight_2()
    forward(2, 2)
    forward(0, 3)
    weight_3()
    forward(1, 3)
    forward(3, 1)
    forward(2, 3)
    weight_4()
    deliver(0)
    deliver(1)
    shared(0)
    loads[4].wait()
    compute(0, 0, HALF)
    forward(3, 2)
    shared(1)
    compute(0, HALF, SLOTS)
    deliver(2)
    place(0)
    reduce_1(0)
    compute(1, 0, HALF)
    shared(2)
    forward(3, 3)
    compute(1, HALF, SLOTS)
    place(1)
    reduce_1(1)
    compute(2, 0, HALF)
    reduce_2(0)
    deliver(3)
    compute(2, HALF, SLOTS)
    place(2)
    reduce_1(2)
    shared(3)
    compute(3, 0, HALF)
    reduce_2(1)
    reduce_3(0)
    compute(3, HALF, SLOTS)
    place(3)
    reduce_1(3)
    reduce_2(2)
    line_end(0)
    reduce_3(1)
    line_end(3)
    reduce_4(0)
    line_end(1)
    line_end(2)
    weight_5()
    reduce_2(3)
    reduce_3(2)
    reduce_4(1)
    weight_6()
    reduce_3(3)
    reduce_5(0)
    reduce_4(2)
    weight_7()
    reduce_4(3)
    reduce_5(1)
    weight_8()
    weight_9()
    reduce_5(2)
    reduce_5(3)


def on_device(
    grad_out, relu_mask, aggregated, weight, adjacency_tiles, tile_rows, tile_cols, tile_count
):
    smem = pl.BlockSpec(memory_space=pltpu.SMEM)
    vmem = pl.BlockSpec(memory_space=pltpu.VMEM)
    hbm = pl.BlockSpec(memory_space=pltpu.HBM)
    bf = lambda *shape: pltpu.VMEM(shape, BF16)
    each = lambda make: tuple(make(width) for width in CHUNKS)
    two = lambda times: each(lambda width: bf(2, times * width, T))
    node_t, wgrad = pl.pallas_call(
        kernel,
        out_shape=(
            jax.ShapeDtypeStruct((512, T), BF16),
            jax.ShapeDtypeStruct((512, 512), BF16),
        ),
        in_specs=[smem, vmem, vmem, hbm, hbm, hbm, hbm, hbm],
        out_specs=(vmem, vmem),
        scratch_shapes=[
            bf(T, 512), pltpu.VMEM((T, 512), jnp.int32), bf(T, 512), bf(512, 512),
            bf(SLOTS, T, T), bf(SLOTS, T, T), pltpu.VMEM((T, T), F32),
            each(lambda width: bf(16, width, T)),
            two(16), two(4), two(4), two(2), two(2), two(4), two(3), two(1),
            each(lambda width: bf(width, T)),
            bf(2, 4, 256, T), bf(4, 256, T), bf(1024, T), bf(768, T),
            bf(256, T), bf(192, T),
            bf(64, T), bf(3, 16, T), bf(4, 16, T), bf(2, 4, 4, 64, T),
            pltpu.VMEM((8, T), jnp.int32), pltpu.VMEM((8, T), jnp.int32), pltpu.VMEM((8, T), F32),
            pltpu.SMEM((8, T), jnp.int32), pltpu.SMEM((8, T), F32),
            pltpu.SemaphoreType.DMA((SEMS,)),
            pltpu.SemaphoreType.DMA((SEMS,)),
            pltpu.SemaphoreType.DMA((NCHUNK, 8, 4)),
            pltpu.SemaphoreType.DMA((NCHUNK, 8)),
            pltpu.SemaphoreType.DMA((NCHUNK,)),
            pltpu.SemaphoreType.DMA((NCHUNK,)),
            pltpu.SemaphoreType.DMA((7,)),
        ],
        compiler_params=pltpu.CompilerParams(
            collective_id=0, has_side_effects=True, vmem_limit_bytes=60 * 1024 * 1024
        ),
        cost_estimate=pl.CostEstimate(flops=1_600_000_000, bytes_accessed=5_000_000, transcendentals=0),
    )(
        tile_count, tile_rows.reshape(1, SLOTS), tile_cols.reshape(1, SLOTS),
        grad_out, relu_mask, aggregated, weight, adjacency_tiles,
    )
    return (node_t.T, wgrad.astype(F32))


def solution(mesh):
    return jax.shard_map(
        on_device,
        mesh=mesh,
        in_specs=(
            P(("row", "col", "depth"), None),
            P(("row", "col", "depth"), None),
            P(("row", "col", "depth"), None),
            P(),
            P(("row", "col", "depth"), None, None),
            P(("row", "col", "depth")),
            P(("row", "col", "depth")),
            P(("row", "col", "depth")),
        ),
        out_specs=(P(("row", "col", "depth"), None), P()),
        check_vma=False,
    )
```

```python
import jax
import jax.numpy as jnp
from jax import lax
from jax.experimental import pallas as pl
from jax.experimental.pallas import tpu as pltpu
from jax.sharding import PartitionSpec as P

MESH = pl.DeviceIdType.MESH
F32 = jnp.float32
BF16 = jnp.bfloat16
T = 128
CHUNKS = (128, 128, 128, 128)
NCHUNK = len(CHUNKS)
STARTS = tuple(sum(CHUNKS[:c]) for c in range(NCHUNK))
SLOTS = 84
GROUP = 32
UNROLL = 6
HALF = SLOTS // 2
SEMS = 112


def wrap4(value):
    return lax.rem(value, 4)


class Ring:
    def __init__(self, k, src, unit, rl, rr, fl, fr, out, right, left):
        self.src, self.unit, self.out = src, unit, out
        self.rl, self.rr, self.fl, self.fr = rl, rr, fl, fr
        u = unit
        self.to_right = k.copy(src.at[pl.ds(3 * u, 2 * u)], rl, right)
        self.to_left = k.copy(src.at[pl.ds(5 * u, 2 * u)], rr, left)
        self.sum_right = k.copy(src.at[pl.ds(2 * u, u)], fl, right)
        self.sum_left = k.copy(src.at[pl.ds(7 * u, u)], fr, left)

    def first(self):
        self.to_right.start()
        self.to_left.start()

    def settle(self):
        for sent in (self.to_right, self.to_left, self.sum_right, self.sum_left):
            sent.wait_send()

    def second(self):
        u, src = self.unit, self.src
        self.to_right.wait_recv()
        src[pl.ds(2 * u, u)] = (
            src[pl.ds(2 * u, u)].astype(F32) + self.rl[pl.ds(u, u)].astype(F32)
        ).astype(BF16)
        self.sum_right.start()
        self.to_left.wait_recv()
        src[pl.ds(7 * u, u)] = (
            src[pl.ds(7 * u, u)].astype(F32) + self.rr[pl.ds(0, u)].astype(F32)
        ).astype(BF16)
        self.sum_left.start()

    def last(self):
        u, src = self.unit, self.src
        self.sum_right.wait_recv()
        self.out[pl.ds(0, u)] = (
            src[pl.ds(0, u)].astype(F32)
            + self.fl[...].astype(F32)
            + self.rr[pl.ds(u, u)].astype(F32)
        ).astype(BF16)
        self.sum_left.wait_recv()
        self.out[pl.ds(u, u)] = (
            src[pl.ds(u, u)].astype(F32)
            + self.rl[pl.ds(0, u)].astype(F32)
            + self.fr[...].astype(F32)
        ).astype(BF16)


class Fan:
    def __init__(self, k, src, unit, landed, devices):
        self.src, self.unit, self.landed = src, unit, landed
        self.sends = [
            k.copy(src.at[pl.ds(s * unit, unit)], landed.at[pl.ds((s - 1) * unit, unit)], devices[s - 1])
            for s in (1, 2, 3)
        ]

    def first(self):
        for s in (1, 0, 2):
            self.sends[s].start()

    def settle(self):
        for sent in self.sends:
            sent.wait_send()

    def arrived(self):
        for sent in self.sends:
            sent.wait_recv()

    def total(self):
        u = self.unit
        value = self.src[pl.ds(0, u)].astype(F32)
        for s in range(3):
            value = value + self.landed[pl.ds(s * u, u)].astype(F32)
        return value


class Copies:
    def __init__(self, send_sems, recv_sems):
        self.send_sems, self.recv_sems, self.used = send_sems, recv_sems, 0

    def copy(self, src, dst, device):
        index = self.used
        self.used += 1
        made = pltpu.make_async_remote_copy(
            src_ref=src,
            dst_ref=dst,
            send_sem=self.send_sems.at[index],
            recv_sem=self.recv_sems.at[index],
            device_id=device,
            device_id_type=MESH,
        )
        return made

    def swap(self, src, dst, device):
        sent = self.copy(src, src, device)
        came = pltpu.make_async_remote_copy(
            src_ref=dst,
            dst_ref=dst,
            send_sem=self.send_sems.at[self.used - 1],
            recv_sem=self.recv_sems.at[self.used - 1],
            device_id=device,
            device_id_type=MESH,
        )
        return sent, came


def kernel(
    count_ref, rows_ref, cols_ref, grad_hbm, mask_hbm, agg_hbm, weight_hbm, tiles_hbm,
    node_ref, wgrad_ref,
    grad_v, mask_v, agg_v, weight_v,
    tiles, seg, acc_ref,
    gathered, parts, xl, xr, xfl, xfr, mids, landed, tops, ztop,
    wl, ws, wa, wxd, wb, wyd, wc, wq, wn, wg,
    lists, places, gates, place_s, gate_s,
    send_sems, recv_sems, line_send, line_recv, share_send, share_recv, local_sems,
):
    row, col, depth = lax.axis_index("row"), lax.axis_index("col"), lax.axis_index("depth")
    x, y = lax.div(row, 4), lax.rem(row, 4)
    z, core = lax.div(col, 2), lax.rem(col, 2)
    zz = depth * 8 + z
    quad = lax.rem(z, 4)
    quads = lax.div(zz, 4)

    def device(dx=0, dy=0):
        return (wrap4(x + dx) * 4 + wrap4(y + dy), col, depth)

    def along_z(step):
        place = lax.rem(zz + step, 16)
        return (row, lax.rem(place, 8) * 2 + core, lax.div(place, 8))

    def in_quad(step):
        return (row, (z - quad + wrap4(quad + step)) * 2 + core, depth)

    sibling = (row, z * 2 + 1 - core, depth)
    right_x, left_x = device(dx=1), device(dx=3)
    right_y, left_y = device(dy=1), device(dy=3)
    all_x = [device(dx=s) for s in (1, 2, 3)]
    all_y = [device(dy=s) for s in (1, 2, 3)]
    partner = (row, col, 1 - depth)
    k = Copies(send_sems, recv_sems)

    loads = [
        pltpu.make_async_copy(src, dst, local_sems.at[i])
        for i, (src, dst) in enumerate((
            (grad_hbm, grad_v), (mask_hbm, mask_v), (weight_hbm, weight_v), (agg_hbm, agg_v), (tiles_hbm, tiles),
        ))
    ]
    for load in loads:
        load.start()

    barrier = pltpu.get_barrier_semaphore()
    peers = [sibling] + all_x + all_y + [along_z(s) for s in (1, 15, 2, 14, 4, 8, 12)]
    peers += [in_quad(s) for s in (1, 2, 3)]
    for peer in peers:
        pl.semaphore_signal(barrier, inc=1, device_id=peer, device_id_type=MESH)

    for load in loads[:3]:
        load.wait()
    grad_v[...] = grad_v[...] * mask_v[...].astype(F32).astype(BF16)
    own = core * 8 + z
    for c in range(NCHUNK):
        gathered[c][own] = lax.dot_general(
            weight_v[pl.ds(STARTS[c], CHUNKS[c]), :], grad_v[...], (((1,), (1,)), ((), ())),
            preferred_element_type=F32,
        ).astype(BF16)
    pl.semaphore_wait(barrier, len(peers))

    def there(place):
        return (place >= 0) & (place <= 7)

    def line(c, source, sign, hop, device=None):
        block = gathered[c].at[core * 8 + source]
        return pltpu.make_async_remote_copy(
            src_ref=block, dst_ref=block,
            send_sem=line_send.at[c, source, hop + (1 if sign > 0 else -1)],
            recv_sem=line_recv.at[c, source],
            device_id=device or (row, (z + sign * hop) * 2 + core, depth), device_id_type=MESH,
        )

    def share(c, side):
        half = gathered[c].at[pl.ds(side * 8, 8)]
        return pltpu.make_async_remote_copy(
            src_ref=half, dst_ref=half,
            send_sem=share_send.at[c], recv_sem=share_recv.at[c],
            device_id=sibling, device_id_type=MESH,
        )

    def each_send(c, source, sign, act):
        for hop in (2, 1):
            @pl.when(there(z + sign * hop))
            def _():
                act(line(c, source, sign, hop))

    def begin(c):
        for sign in (1, -1):
            each_send(c, z, sign, lambda made: made.start())

    def forward(c, m):
        for sign in (1, -1):
            source = z - sign * 2 * m

            @pl.when(there(source))
            def _():
                line(c, source, sign, 1, sibling).wait_recv()
                each_send(c, source, sign, lambda made: made.start())

    def deliver(c):
        for m in range(4):
            for sign in (1, -1):
                source = z - sign * (2 * m + 1)

                @pl.when(there(source))
                def _():
                    line(c, source, sign, 1, sibling).wait_recv()
        share(c, core).start()

    def shared(c):
        share(c, 1 - core).wait_recv()

    def line_end(c):
        for m in range(4):
            for sign in (1, -1):
                source = z - sign * 2 * m

                @pl.when(there(source))
                def _():
                    each_send(c, source, sign, lambda made: made.wait_send())
        share(c, core).wait_send()

    w_share = k.copy(wl.at[1 - core], ws, sibling)
    w_x = Fan(k, wa, 256, wxd, all_x)
    w_y = Fan(k, wb, 64, wyd, all_y)
    w_q = [
        k.copy(wc.at[pl.ds(pl.multiple_of(wrap4(quad + s) * 16, 16), 16)], wq.at[s - 1], in_quad(s))
        for s in (1, 2, 3)
    ]
    w_n = [
        k.swap(wn.at[quads], wn.at[wrap4(quads + 4 - s)], along_z(4 * s)) for s in (1, 2, 3)
    ]

    def strip(place):
        return wg.at[core, x, y, pl.ds(pl.multiple_of(place * 16, 16), 16)]

    w_back_q = [k.swap(strip(quad), strip(wrap4(quad + 4 - s)), in_quad(s)) for s in (1, 2, 3)]
    w_back_y = [
        k.swap(wg.at[core, x, y], wg.at[core, x, wrap4(y + 4 - s)], device(dy=s)) for s in (1, 2, 3)
    ]
    w_back_x = [
        k.swap(wg.at[core, x], wg.at[core, wrap4(x + 4 - s)], device(dx=s)) for s in (1, 2, 3)
    ]
    w_back_core = k.swap(wg.at[core], wg.at[1 - core], sibling)

    def weight_0():
        loads[3].wait()
        for h in range(2):
            for q in range(4):
                wl[h, q] = lax.dot_general(
                    agg_v[:, h * 256:(h + 1) * 256], grad_v[:, q * T:(q + 1) * T],
                    (((0,), (0,)), ((), ())), preferred_element_type=F32,
                ).astype(BF16)
        w_share.start()

    def weight_1():
        w_share.wait_recv()
        for a in range(4):
            xt = wrap4(x + a)
            for b in range(4):
                rows = pl.ds(pl.multiple_of(wrap4(y + b) * 64, 64), 64)
                wa[pl.ds(a * 256 + b * 64, 64)] = (
                    wl[core, xt, rows].astype(F32) + ws[xt, rows].astype(F32)
                ).astype(BF16)
        w_x.first()
        w_share.wait_send()

    def weight_2():
        w_x.arrived()
        wb[...] = w_x.total().astype(BF16)
        w_y.first()
        w_x.settle()

    def weight_3():
        w_y.arrived()
        wc[...] = w_y.total().astype(BF16)
        for sent in w_q:
            sent.start()
        w_y.settle()

    def weight_4():
        total = wc[pl.ds(pl.multiple_of(quad * 16, 16), 16)].astype(F32)
        for s in range(3):
            w_q[s].wait_recv()
            total = total + wq[s].astype(F32)
        wn[quads] = total.astype(BF16)
        for sent, _ in w_n:
            sent.start()
        for sent in w_q:
            sent.wait_send()

    def weight_5():
        for _, came in w_n:
            came.wait_recv()
        total = wn[0].astype(F32)
        for place in range(1, 4):
            total = total + wn[place].astype(F32)
        wg[core, x, y, pl.ds(pl.multiple_of(quad * 16, 16), 16)] = total.astype(BF16)
        for sent, _ in w_back_q:
            sent.start()
        for sent, _ in w_n:
            sent.wait_send()

    def weight_6():
        for _, came in w_back_q:
            came.wait_recv()
        for sent, _ in w_back_y:
            sent.start()
        for sent, _ in w_back_q:
            sent.wait_send()

    def weight_7():
        for _, came in w_back_y:
            came.wait_recv()
        for sent, _ in w_back_x:
            sent.start()
        for sent, _ in w_back_y:
            sent.wait_send()

    def weight_8():
        for _, came in w_back_x:
            came.wait_recv()
        w_back_core[0].start()
        for sent, _ in w_back_x:
            sent.wait_send()

    def weight_9():
        w_back_core[1].wait_recv()
        w_back_core[0].wait_send()
        for h in range(2):
            for a in range(4):
                for b in range(4):
                    wgrad_ref[pl.ds(h * 256 + b * 64, 64), a * T:(a + 1) * T] = wg[h, a, b]

    def sort():
        lane = lax.broadcasted_iota(jnp.int32, (1, T), 1)
        lists[...] = jnp.zeros((8, T), jnp.int32)
        lists[0:1, 0:SLOTS] = cols_ref[...]
        lists[1:2, 0:SLOTS] = rows_ref[...]
        key = jnp.where(lane < count_ref[0], lists[0:1, :], GROUP)
        key = jnp.where(lane < SLOTS, key, GROUP)
        tile_row = lists[1:2, :]
        slab_place = (tile_row & 1) * 8 + (tile_row >> 1)
        above = lax.broadcasted_iota(jnp.int32, (T, T), 0)
        across = lax.broadcasted_iota(jnp.int32, (T, T), 1)

        def wide(value):
            return jnp.broadcast_to(value, (T, T))

        def count(mask, value=1):
            return jnp.sum(jnp.where(mask, value, 0), axis=0, keepdims=True)

        key_a = wide(key)
        key_t = key_a.T
        same = (key_t == key_a) & (above < across)
        rank = count((key_t < key_a) | same)
        follows = jnp.minimum(count(same), 1)
        chosen = wide(rank).T == across
        places[0:1, :] = jnp.minimum(count(chosen, above), SLOTS - 1)
        places[1:2, :] = jnp.minimum(count(chosen, wide(slab_place).T), 15)
        places[2:3, :] = jnp.clip(count(key_t <= across) - 1, 0, SLOTS - 1)
        gates[0:1, :] = count(chosen, wide(follows).T).astype(F32)
        gates[1:2, :] = jnp.minimum(count(key_t == across), 1).astype(F32)
        for made in (
            pltpu.make_async_copy(places, place_s, local_sems.at[5]),
            pltpu.make_async_copy(gates, gate_s, local_sems.at[6]),
        ):
            made.start()
            made.wait()

    def compute(c, first, stop):
        width = CHUNKS[c]

        def block(step, acc):
            for inner in range(UNROLL):
                p = first + step * UNROLL + inner
                product = jnp.dot(
                    gathered[c][place_s[1, p]], tiles[place_s[0, p]],
                    preferred_element_type=F32,
                )
                acc = acc * gate_s[0, p] + product
                seg[p, 0:width] = acc.astype(BF16)
            return acc

        if first == 0:
            start = jnp.zeros((width, T), F32)
        else:
            start = acc_ref[0:width]
        end = lax.fori_loop(0, (stop - first) // UNROLL, block, start)
        if stop < SLOTS:
            acc_ref[0:width] = end

    def place(c):
        width = CHUNKS[c]

        def one(m, carry):
            major, minor = lax.div(m, 4), lax.rem(m, 4)
            rows = pl.ds(pl.multiple_of(m * width, width), width)
            for dt in range(2):
                a, b = (major, minor) if dt == 0 else (minor, major)
                target = (wrap4(x + a) * 4 + wrap4(y + b)) * 2 + dt
                parts[c][dt, rows] = (
                    seg[place_s[2, target], 0:width].astype(F32) * gate_s[1, target]
                ).astype(BF16)
            return carry

        lax.fori_loop(0, 16, one, 0)

    ring, fan, cross = [], [], []
    for c in range(NCHUNK):
        for dt in range(2):
            far = (right_x, left_x) if dt == 0 else (right_y, left_y)
            ring.append(Ring(
                k, parts[c].at[dt], 2 * CHUNKS[c],
                xl[c].at[dt], xr[c].at[dt], xfl[c].at[dt], xfr[c].at[dt], mids[c].at[dt], *far,
            ))
            fan.append(Fan(
                k, mids[c].at[dt], CHUNKS[c], landed[c].at[dt], all_y if dt == 0 else all_x
            ))
        cross.append(k.copy(tops[c].at[1 - depth], ztop[c], partner))

    def reduce_1(c):
        for dt in range(2):
            ring[2 * c + dt].first()

    def reduce_2(c):
        for dt in range(2):
            ring[2 * c + dt].second()

    def reduce_3(c):
        for dt in range(2):
            ring[2 * c + dt].last()
            fan[2 * c + dt].first()
        for dt in range(2):
            ring[2 * c + dt].settle()

    def reduce_4(c):
        for dt in range(2):
            fan[2 * c + dt].arrived()
        width = CHUNKS[c]
        for turn, dt in enumerate((1 - depth, depth)):
            total = mids[c][dt, 0:width].astype(F32)
            for s in range(3):
                total = total + landed[c][dt, s * width:(s + 1) * width].astype(F32)
            tops[c][dt] = total.astype(BF16)
            if turn == 0:
                cross[c].start()
        for dt in range(2):
            fan[2 * c + dt].settle()

    def reduce_5(c):
        cross[c].wait_send()
        cross[c].wait_recv()
        node_ref[pl.ds(STARTS[c], CHUNKS[c])] = (
            tops[c][depth].astype(F32) + ztop[c][...].astype(F32)
        ).astype(BF16)

    begin(0)
    sort()
    begin(1)
    begin(2)
    weight_0()
    forward(0, 1)
    weight_1()
    forward(1, 1)
    forward(2, 1)
    forward(0, 2)
    forward(1, 2)
    begin(3)
    weight_2()
    forward(2, 2)
    forward(0, 3)
    weight_3()
    forward(1, 3)
    forward(3, 1)
    forward(2, 3)
    weight_4()
    deliver(0)
    deliver(1)
    shared(0)
    loads[4].wait()
    compute(0, 0, HALF)
    forward(3, 2)
    shared(1)
    compute(0, HALF, SLOTS)
    deliver(2)
    place(0)
    reduce_1(0)
    compute(1, 0, HALF)
    shared(2)
    forward(3, 3)
    compute(1, HALF, SLOTS)
    place(1)
    reduce_1(1)
    compute(2, 0, HALF)
    reduce_2(0)
    deliver(3)
    compute(2, HALF, SLOTS)
    place(2)
    reduce_1(2)
    shared(3)
    compute(3, 0, HALF)
    reduce_2(1)
    reduce_3(0)
    compute(3, HALF, SLOTS)
    place(3)
    reduce_1(3)
    reduce_2(2)
    line_end(0)
    reduce_3(1)
    line_end(3)
    reduce_4(0)
    line_end(1)
    line_end(2)
    weight_5()
    reduce_2(3)
    reduce_3(2)
    reduce_4(1)
    weight_6()
    reduce_3(3)
    reduce_5(0)
    reduce_4(2)
    weight_7()
    reduce_4(3)
    reduce_5(1)
    weight_8()
    weight_9()
    reduce_5(2)
    reduce_5(3)


def finish(node_t_ref, wgrad_t_ref, node_ref, wgrad_ref):
    for q in range(4):
        node_ref[:, q * T:(q + 1) * T] = node_t_ref[q * T:(q + 1) * T].astype(F32).T.astype(BF16)
    wgrad_ref[...] = wgrad_t_ref[...].astype(F32)


def on_device(
    grad_out, relu_mask, aggregated, weight, adjacency_tiles, tile_rows, tile_cols, tile_count
):
    smem = pl.BlockSpec(memory_space=pltpu.SMEM)
    vmem = pl.BlockSpec(memory_space=pltpu.VMEM)
    hbm = pl.BlockSpec(memory_space=pltpu.HBM)
    bf = lambda *shape: pltpu.VMEM(shape, BF16)
    each = lambda make: tuple(make(width) for width in CHUNKS)
    two = lambda times: each(lambda width: bf(2, times * width, T))
    node_t, wgrad = pl.pallas_call(
        kernel,
        out_shape=(
            jax.ShapeDtypeStruct((512, T), BF16),
            jax.ShapeDtypeStruct((512, 512), BF16),
        ),
        in_specs=[smem, vmem, vmem, hbm, hbm, hbm, hbm, hbm],
        out_specs=(vmem, vmem),
        scratch_shapes=[
            bf(T, 512), pltpu.VMEM((T, 512), jnp.int32), bf(T, 512), bf(512, 512),
            bf(SLOTS, T, T), bf(SLOTS, T, T), pltpu.VMEM((T, T), F32),
            each(lambda width: bf(16, width, T)),
            two(16), two(4), two(4), two(2), two(2), two(4), two(3), two(1),
            each(lambda width: bf(width, T)),
            bf(2, 4, 256, T), bf(4, 256, T), bf(1024, T), bf(768, T),
            bf(256, T), bf(192, T),
            bf(64, T), bf(3, 16, T), bf(4, 16, T), bf(2, 4, 4, 64, T),
            pltpu.VMEM((8, T), jnp.int32), pltpu.VMEM((8, T), jnp.int32), pltpu.VMEM((8, T), F32),
            pltpu.SMEM((8, T), jnp.int32), pltpu.SMEM((8, T), F32),
            pltpu.SemaphoreType.DMA((SEMS,)),
            pltpu.SemaphoreType.DMA((SEMS,)),
            pltpu.SemaphoreType.DMA((NCHUNK, 8, 4)),
            pltpu.SemaphoreType.DMA((NCHUNK, 8)),
            pltpu.SemaphoreType.DMA((NCHUNK,)),
            pltpu.SemaphoreType.DMA((NCHUNK,)),
            pltpu.SemaphoreType.DMA((7,)),
        ],
        compiler_params=pltpu.CompilerParams(
            collective_id=0, has_side_effects=True, vmem_limit_bytes=60 * 1024 * 1024
        ),
        cost_estimate=pl.CostEstimate(flops=1_600_000_000, bytes_accessed=5_000_000, transcendentals=0),
    )(
        tile_count, tile_rows.reshape(1, SLOTS), tile_cols.reshape(1, SLOTS),
        grad_out, relu_mask, aggregated, weight, adjacency_tiles,
    )
    return pl.pallas_call(
        finish,
        out_shape=(
            jax.ShapeDtypeStruct((T, 512), BF16),
            jax.ShapeDtypeStruct((512, 512), F32),
        ),
        in_specs=[vmem, vmem],
        out_specs=(vmem, vmem),
        cost_estimate=pl.CostEstimate(flops=300_000, bytes_accessed=1_900_000, transcendentals=0),
    )(node_t, wgrad)


def solution(mesh):
    return jax.shard_map(
        on_device,
        mesh=mesh,
        in_specs=(
            P(("row", "col", "depth"), None),
            P(("row", "col", "depth"), None),
            P(("row", "col", "depth"), None),
            P(),
            P(("row", "col", "depth"), None, None),
            P(("row", "col", "depth")),
            P(("row", "col", "depth")),
            P(("row", "col", "depth")),
        ),
        out_specs=(P(("row", "col", "depth"), None), P()),
        check_vma=False,
    )
```

```python
import jax
import jax.numpy as jnp
from jax import lax
from jax.experimental import pallas as pl
from jax.experimental.pallas import tpu as pltpu
from jax.sharding import PartitionSpec as P

MESH = pl.DeviceIdType.MESH
F32 = jnp.float32
BF16 = jnp.bfloat16
T = 128
CHUNKS = (128, 128, 128, 128)
NCHUNK = len(CHUNKS)
STARTS = tuple(sum(CHUNKS[:c]) for c in range(NCHUNK))
SLOTS = 84
GROUP = 32
UNROLL = 6
HALF = SLOTS // 2
SEMS = 112


def wrap4(value):
    return lax.rem(value, 4)


class Ring:
    def __init__(self, k, src, unit, rl, rr, fl, fr, out, right, left):
        self.src, self.unit, self.out = src, unit, out
        self.rl, self.rr, self.fl, self.fr = rl, rr, fl, fr
        u = unit
        self.to_right = k.copy(src.at[pl.ds(3 * u, 2 * u)], rl, right)
        self.to_left = k.copy(src.at[pl.ds(5 * u, 2 * u)], rr, left)
        self.sum_right = k.copy(src.at[pl.ds(2 * u, u)], fl, right)
        self.sum_left = k.copy(src.at[pl.ds(7 * u, u)], fr, left)

    def first(self):
        self.to_right.start()
        self.to_left.start()

    def settle(self):
        for sent in (self.to_right, self.to_left, self.sum_right, self.sum_left):
            sent.wait_send()

    def second(self):
        u, src = self.unit, self.src
        self.to_right.wait_recv()
        src[pl.ds(2 * u, u)] = (
            src[pl.ds(2 * u, u)].astype(F32) + self.rl[pl.ds(u, u)].astype(F32)
        ).astype(BF16)
        self.sum_right.start()
        self.to_left.wait_recv()
        src[pl.ds(7 * u, u)] = (
            src[pl.ds(7 * u, u)].astype(F32) + self.rr[pl.ds(0, u)].astype(F32)
        ).astype(BF16)
        self.sum_left.start()

    def last(self):
        u, src = self.unit, self.src
        self.sum_right.wait_recv()
        self.out[pl.ds(0, u)] = (
            src[pl.ds(0, u)].astype(F32)
            + self.fl[...].astype(F32)
            + self.rr[pl.ds(u, u)].astype(F32)
        ).astype(BF16)
        self.sum_left.wait_recv()
        self.out[pl.ds(u, u)] = (
            src[pl.ds(u, u)].astype(F32)
            + self.rl[pl.ds(0, u)].astype(F32)
            + self.fr[...].astype(F32)
        ).astype(BF16)


class Fan:
    def __init__(self, k, src, unit, landed, devices):
        self.src, self.unit, self.landed = src, unit, landed
        self.sends = [
            k.copy(src.at[pl.ds(s * unit, unit)], landed.at[pl.ds((s - 1) * unit, unit)], devices[s - 1])
            for s in (1, 2, 3)
        ]

    def first(self):
        for s in (1, 0, 2):
            self.sends[s].start()

    def settle(self):
        for sent in self.sends:
            sent.wait_send()

    def arrived(self):
        for sent in self.sends:
            sent.wait_recv()

    def total(self):
        u = self.unit
        value = self.src[pl.ds(0, u)].astype(F32)
        for s in range(3):
            value = value + self.landed[pl.ds(s * u, u)].astype(F32)
        return value


class Copies:
    def __init__(self, send_sems, recv_sems):
        self.send_sems, self.recv_sems, self.used = send_sems, recv_sems, 0

    def copy(self, src, dst, device):
        index = self.used
        self.used += 1
        made = pltpu.make_async_remote_copy(
            src_ref=src,
            dst_ref=dst,
            send_sem=self.send_sems.at[index],
            recv_sem=self.recv_sems.at[index],
            device_id=device,
            device_id_type=MESH,
        )
        return made

    def swap(self, src, dst, device):
        sent = self.copy(src, src, device)
        came = pltpu.make_async_remote_copy(
            src_ref=dst,
            dst_ref=dst,
            send_sem=self.send_sems.at[self.used - 1],
            recv_sem=self.recv_sems.at[self.used - 1],
            device_id=device,
            device_id_type=MESH,
        )
        return sent, came


def kernel(
    count_ref, rows_ref, cols_ref, grad_hbm, mask_hbm, agg_hbm, weight_hbm, tiles_hbm,
    node_ref, wgrad_ref,
    grad_v, mask_v, agg_v, weight_v,
    tiles, seg, acc_ref,
    gathered, parts, xl, xr, xfl, xfr, mids, landed, tops, ztop,
    wl, ws, wa, wxd, wb, wyd, wc, wq, wn, wg,
    lists, places, gates, place_s, gate_s,
    send_sems, recv_sems, line_send, line_recv, share_send, share_recv, local_sems,
):
    row, col, depth = lax.axis_index("row"), lax.axis_index("col"), lax.axis_index("depth")
    x, y = lax.div(row, 4), lax.rem(row, 4)
    z, core = lax.div(col, 2), lax.rem(col, 2)
    zz = depth * 8 + z
    quad = lax.rem(z, 4)
    quads = lax.div(zz, 4)

    def device(dx=0, dy=0):
        return (wrap4(x + dx) * 4 + wrap4(y + dy), col, depth)

    def along_z(step):
        place = lax.rem(zz + step, 16)
        return (row, lax.rem(place, 8) * 2 + core, lax.div(place, 8))

    def in_quad(step):
        return (row, (z - quad + wrap4(quad + step)) * 2 + core, depth)

    sibling = (row, z * 2 + 1 - core, depth)
    right_x, left_x = device(dx=1), device(dx=3)
    right_y, left_y = device(dy=1), device(dy=3)
    all_x = [device(dx=s) for s in (1, 2, 3)]
    all_y = [device(dy=s) for s in (1, 2, 3)]
    partner = (row, col, 1 - depth)
    k = Copies(send_sems, recv_sems)

    loads = [
        pltpu.make_async_copy(src, dst, local_sems.at[i])
        for i, (src, dst) in enumerate((
            (grad_hbm, grad_v), (mask_hbm, mask_v), (weight_hbm, weight_v), (agg_hbm, agg_v), (tiles_hbm, tiles),
        ))
    ]
    for load in loads:
        load.start()

    barrier = pltpu.get_barrier_semaphore()
    peers = [sibling] + all_x + all_y + [along_z(s) for s in (1, 15, 2, 14, 4, 8, 12)]
    peers += [in_quad(s) for s in (1, 2, 3)]
    for peer in peers:
        pl.semaphore_signal(barrier, inc=1, device_id=peer, device_id_type=MESH)

    for load in loads[:3]:
        load.wait()
    grad_v[...] = grad_v[...] * mask_v[...].astype(F32).astype(BF16)
    own = core * 8 + z
    for c in range(NCHUNK):
        gathered[c][own] = lax.dot_general(
            weight_v[pl.ds(STARTS[c], CHUNKS[c]), :], grad_v[...], (((1,), (1,)), ((), ())),
            preferred_element_type=F32,
        ).astype(BF16)
    pl.semaphore_wait(barrier, len(peers))

    def there(place):
        return (place >= 0) & (place <= 7)

    def line(c, source, sign, hop, device=None):
        block = gathered[c].at[core * 8 + source]
        return pltpu.make_async_remote_copy(
            src_ref=block, dst_ref=block,
            send_sem=line_send.at[c, source, hop + (1 if sign > 0 else -1)],
            recv_sem=line_recv.at[c, source],
            device_id=device or (row, (z + sign * hop) * 2 + core, depth), device_id_type=MESH,
        )

    def share(c, side):
        half = gathered[c].at[pl.ds(side * 8, 8)]
        return pltpu.make_async_remote_copy(
            src_ref=half, dst_ref=half,
            send_sem=share_send.at[c], recv_sem=share_recv.at[c],
            device_id=sibling, device_id_type=MESH,
        )

    def each_send(c, source, sign, act):
        for hop in (2, 1):
            @pl.when(there(z + sign * hop))
            def _():
                act(line(c, source, sign, hop))

    def begin(c):
        for sign in (1, -1):
            each_send(c, z, sign, lambda made: made.start())

    def forward(c, m):
        for sign in (1, -1):
            source = z - sign * 2 * m

            @pl.when(there(source))
            def _():
                line(c, source, sign, 1, sibling).wait_recv()
                each_send(c, source, sign, lambda made: made.start())

    def deliver(c):
        for m in range(4):
            for sign in (1, -1):
                source = z - sign * (2 * m + 1)

                @pl.when(there(source))
                def _():
                    line(c, source, sign, 1, sibling).wait_recv()
        share(c, core).start()

    def shared(c):
        share(c, 1 - core).wait_recv()

    def line_end(c):
        for m in range(4):
            for sign in (1, -1):
                source = z - sign * 2 * m

                @pl.when(there(source))
                def _():
                    each_send(c, source, sign, lambda made: made.wait_send())
        share(c, core).wait_send()

    w_share = k.copy(wl.at[1 - core], ws, sibling)
    w_x = Fan(k, wa, 256, wxd, all_x)
    w_y = Fan(k, wb, 64, wyd, all_y)
    w_q = [
        k.copy(wc.at[pl.ds(pl.multiple_of(wrap4(quad + s) * 16, 16), 16)], wq.at[s - 1], in_quad(s))
        for s in (1, 2, 3)
    ]
    w_n = [
        k.swap(wn.at[quads], wn.at[wrap4(quads + 4 - s)], along_z(4 * s)) for s in (1, 2, 3)
    ]

    def strip(place):
        return wg.at[core, x, y, pl.ds(pl.multiple_of(place * 16, 16), 16)]

    w_back_q = [k.swap(strip(quad), strip(wrap4(quad + 4 - s)), in_quad(s)) for s in (1, 2, 3)]
    w_back_y = [
        k.swap(wg.at[core, x, y], wg.at[core, x, wrap4(y + 4 - s)], device(dy=s)) for s in (1, 2, 3)
    ]
    w_back_x = [
        k.swap(wg.at[core, x], wg.at[core, wrap4(x + 4 - s)], device(dx=s)) for s in (1, 2, 3)
    ]
    w_back_core = k.swap(wg.at[core], wg.at[1 - core], sibling)

    def weight_0():
        loads[3].wait()
        for h in range(2):
            for q in range(4):
                wl[h, q] = lax.dot_general(
                    agg_v[:, h * 256:(h + 1) * 256], grad_v[:, q * T:(q + 1) * T],
                    (((0,), (0,)), ((), ())), preferred_element_type=F32,
                ).astype(BF16)
        w_share.start()

    def weight_1():
        w_share.wait_recv()
        for a in range(4):
            xt = wrap4(x + a)
            for b in range(4):
                rows = pl.ds(pl.multiple_of(wrap4(y + b) * 64, 64), 64)
                wa[pl.ds(a * 256 + b * 64, 64)] = (
                    wl[core, xt, rows].astype(F32) + ws[xt, rows].astype(F32)
                ).astype(BF16)
        w_x.first()
        w_share.wait_send()

    def weight_2():
        w_x.arrived()
        wb[...] = w_x.total().astype(BF16)
        w_y.first()
        w_x.settle()

    def weight_3():
        w_y.arrived()
        wc[...] = w_y.total().astype(BF16)
        for sent in w_q:
            sent.start()
        w_y.settle()

    def weight_4():
        total = wc[pl.ds(pl.multiple_of(quad * 16, 16), 16)].astype(F32)
        for s in range(3):
            w_q[s].wait_recv()
            total = total + wq[s].astype(F32)
        wn[quads] = total.astype(BF16)
        for sent, _ in w_n:
            sent.start()
        for sent in w_q:
            sent.wait_send()

    def weight_5():
        for _, came in w_n:
            came.wait_recv()
        total = wn[0].astype(F32)
        for place in range(1, 4):
            total = total + wn[place].astype(F32)
        wg[core, x, y, pl.ds(pl.multiple_of(quad * 16, 16), 16)] = total.astype(BF16)
        for sent, _ in w_back_q:
            sent.start()
        for sent, _ in w_n:
            sent.wait_send()

    def weight_6():
        for _, came in w_back_q:
            came.wait_recv()
        for sent, _ in w_back_y:
            sent.start()
        for sent, _ in w_back_q:
            sent.wait_send()

    def weight_7():
        for _, came in w_back_y:
            came.wait_recv()
        for sent, _ in w_back_x:
            sent.start()
        for sent, _ in w_back_y:
            sent.wait_send()

    def weight_8():
        for _, came in w_back_x:
            came.wait_recv()
        w_back_core[0].start()
        for sent, _ in w_back_x:
            sent.wait_send()

    def weight_9():
        w_back_core[1].wait_recv()
        w_back_core[0].wait_send()
        for h in range(2):
            for a in range(4):
                for b in range(4):
                    wgrad_ref[pl.ds(h * 256 + b * 64, 64), a * T:(a + 1) * T] = wg[h, a, b]

    def sort():
        lane = lax.broadcasted_iota(jnp.int32, (1, T), 1)
        lists[...] = jnp.zeros((8, T), jnp.int32)
        lists[0:1, 0:SLOTS] = cols_ref[...]
        lists[1:2, 0:SLOTS] = rows_ref[...]
        key = jnp.where(lane < count_ref[0], lists[0:1, :], GROUP)
        key = jnp.where(lane < SLOTS, key, GROUP)
        tile_row = lists[1:2, :]
        slab_place = (tile_row & 1) * 8 + (tile_row >> 1)
        above = lax.broadcasted_iota(jnp.int32, (T, T), 0)
        across = lax.broadcasted_iota(jnp.int32, (T, T), 1)

        def wide(value):
            return jnp.broadcast_to(value, (T, T))

        def count(mask, value=1):
            return jnp.sum(jnp.where(mask, value, 0), axis=0, keepdims=True)

        key_a = wide(key)
        key_t = key_a.T
        same = (key_t == key_a) & (above < across)
        rank = count((key_t < key_a) | same)
        follows = jnp.minimum(count(same), 1)
        chosen = wide(rank).T == across
        places[0:1, :] = jnp.minimum(count(chosen, above), SLOTS - 1)
        places[1:2, :] = jnp.minimum(count(chosen, wide(slab_place).T), 15)
        places[2:3, :] = jnp.clip(count(key_t <= across) - 1, 0, SLOTS - 1)
        gates[0:1, :] = count(chosen, wide(follows).T).astype(F32)
        gates[1:2, :] = jnp.minimum(count(key_t == across), 1).astype(F32)
        for made in (
            pltpu.make_async_copy(places, place_s, local_sems.at[5]),
            pltpu.make_async_copy(gates, gate_s, local_sems.at[6]),
        ):
            made.start()
            made.wait()

    def compute(c, first, stop):
        width = CHUNKS[c]

        def block(step, acc):
            for inner in range(UNROLL):
                p = first + step * UNROLL + inner
                product = jnp.dot(
                    gathered[c][place_s[1, p]], tiles[place_s[0, p]],
                    preferred_element_type=F32,
                )
                acc = acc * gate_s[0, p] + product
                seg[p, 0:width] = acc.astype(BF16)
            return acc

        if first == 0:
            start = jnp.zeros((width, T), F32)
        else:
            start = acc_ref[0:width]
        end = lax.fori_loop(0, (stop - first) // UNROLL, block, start)
        if stop < SLOTS:
            acc_ref[0:width] = end

    def place(c):
        width = CHUNKS[c]

        def one(m, carry):
            major, minor = lax.div(m, 4), lax.rem(m, 4)
            rows = pl.ds(pl.multiple_of(m * width, width), width)
            for dt in range(2):
                a, b = (major, minor) if dt == 0 else (minor, major)
                target = (wrap4(x + a) * 4 + wrap4(y + b)) * 2 + dt
                parts[c][dt, rows] = (
                    seg[place_s[2, target], 0:width].astype(F32) * gate_s[1, target]
                ).astype(BF16)
            return carry

        lax.fori_loop(0, 16, one, 0)

    ring, fan, cross = [], [], []
    for c in range(NCHUNK):
        for dt in range(2):
            far = (right_x, left_x) if dt == 0 else (right_y, left_y)
            ring.append(Ring(
                k, parts[c].at[dt], 2 * CHUNKS[c],
                xl[c].at[dt], xr[c].at[dt], xfl[c].at[dt], xfr[c].at[dt], mids[c].at[dt], *far,
            ))
            fan.append(Fan(
                k, mids[c].at[dt], CHUNKS[c], landed[c].at[dt], all_y if dt == 0 else all_x
            ))
        cross.append(k.copy(tops[c].at[1 - depth], ztop[c], partner))

    def reduce_1(c):
        for dt in range(2):
            ring[2 * c + dt].first()

    def reduce_2(c):
        for dt in range(2):
            ring[2 * c + dt].second()

    def reduce_3(c):
        for dt in range(2):
            ring[2 * c + dt].last()
            fan[2 * c + dt].first()
        for dt in range(2):
            ring[2 * c + dt].settle()

    def reduce_4(c):
        for dt in range(2):
            fan[2 * c + dt].arrived()
        width = CHUNKS[c]
        for turn, dt in enumerate((1 - depth, depth)):
            total = mids[c][dt, 0:width].astype(F32)
            for s in range(3):
                total = total + landed[c][dt, s * width:(s + 1) * width].astype(F32)
            tops[c][dt] = total.astype(BF16)
            if turn == 0:
                cross[c].start()
        for dt in range(2):
            fan[2 * c + dt].settle()

    def reduce_5(c):
        cross[c].wait_send()
        cross[c].wait_recv()
        node_ref[pl.ds(STARTS[c], CHUNKS[c])] = (
            tops[c][depth].astype(F32) + ztop[c][...].astype(F32)
        ).astype(BF16)

    begin(0)
    begin(1)
    sort()
    begin(2)
    weight_0()
    forward(0, 1)
    forward(1, 1)
    forward(2, 1)
    forward(0, 2)
    forward(1, 2)
    forward(2, 2)
    forward(0, 3)
    weight_1()
    begin(3)
    forward(1, 3)
    forward(2, 3)
    deliver(0)
    forward(3, 1)
    weight_2()
    shared(0)
    loads[4].wait()
    compute(0, 0, HALF)
    deliver(1)
    compute(0, HALF, SLOTS)
    deliver(2)
    forward(3, 2)
    shared(1)
    place(0)
    reduce_1(0)
    compute(1, 0, HALF)
    compute(1, HALF, SLOTS)
    place(1)
    reduce_1(1)
    forward(3, 3)
    shared(2)
    compute(2, 0, HALF)
    reduce_2(0)
    weight_3()
    line_end(2)
    compute(2, HALF, SLOTS)
    deliver(3)
    place(2)
    reduce_1(2)
    weight_4()
    reduce_2(1)
    reduce_3(0)
    shared(3)
    compute(3, 0, HALF)
    compute(3, HALF, SLOTS)
    place(3)
    reduce_1(3)
    reduce_2(2)
    line_end(3)
    reduce_3(1)
    line_end(0)
    reduce_4(0)
    weight_5()
    line_end(1)
    reduce_2(3)
    reduce_3(2)
    reduce_4(1)
    weight_6()
    reduce_3(3)
    reduce_5(0)
    reduce_4(2)
    weight_7()
    reduce_4(3)
    reduce_5(1)
    weight_8()
    weight_9()
    reduce_5(2)
    reduce_5(3)


def finish(node_t_ref, wgrad_t_ref, node_ref, wgrad_ref):
    for q in range(4):
        node_ref[:, q * T:(q + 1) * T] = node_t_ref[q * T:(q + 1) * T].astype(F32).T.astype(BF16)
    wgrad_ref[...] = wgrad_t_ref[...].astype(F32)


def on_device(
    grad_out, relu_mask, aggregated, weight, adjacency_tiles, tile_rows, tile_cols, tile_count
):
    smem = pl.BlockSpec(memory_space=pltpu.SMEM)
    vmem = pl.BlockSpec(memory_space=pltpu.VMEM)
    hbm = pl.BlockSpec(memory_space=pltpu.HBM)
    bf = lambda *shape: pltpu.VMEM(shape, BF16)
    each = lambda make: tuple(make(width) for width in CHUNKS)
    two = lambda times: each(lambda width: bf(2, times * width, T))
    node_t, wgrad = pl.pallas_call(
        kernel,
        out_shape=(
            jax.ShapeDtypeStruct((512, T), BF16),
            jax.ShapeDtypeStruct((512, 512), BF16),
        ),
        in_specs=[smem, vmem, vmem, hbm, hbm, hbm, hbm, hbm],
        out_specs=(vmem, vmem),
        scratch_shapes=[
            bf(T, 512), pltpu.VMEM((T, 512), jnp.int32), bf(T, 512), bf(512, 512),
            bf(SLOTS, T, T), bf(SLOTS, T, T), pltpu.VMEM((T, T), F32),
            each(lambda width: bf(16, width, T)),
            two(16), two(4), two(4), two(2), two(2), two(4), two(3), two(1),
            each(lambda width: bf(width, T)),
            bf(2, 4, 256, T), bf(4, 256, T), bf(1024, T), bf(768, T),
            bf(256, T), bf(192, T),
            bf(64, T), bf(3, 16, T), bf(4, 16, T), bf(2, 4, 4, 64, T),
            pltpu.VMEM((8, T), jnp.int32), pltpu.VMEM((8, T), jnp.int32), pltpu.VMEM((8, T), F32),
            pltpu.SMEM((8, T), jnp.int32), pltpu.SMEM((8, T), F32),
            pltpu.SemaphoreType.DMA((SEMS,)),
            pltpu.SemaphoreType.DMA((SEMS,)),
            pltpu.SemaphoreType.DMA((NCHUNK, 8, 4)),
            pltpu.SemaphoreType.DMA((NCHUNK, 8)),
            pltpu.SemaphoreType.DMA((NCHUNK,)),
            pltpu.SemaphoreType.DMA((NCHUNK,)),
            pltpu.SemaphoreType.DMA((7,)),
        ],
        compiler_params=pltpu.CompilerParams(
            collective_id=0, has_side_effects=True, vmem_limit_bytes=60 * 1024 * 1024
        ),
        cost_estimate=pl.CostEstimate(flops=1_600_000_000, bytes_accessed=5_000_000, transcendentals=0),
    )(
        tile_count, tile_rows.reshape(1, SLOTS), tile_cols.reshape(1, SLOTS),
        grad_out, relu_mask, aggregated, weight, adjacency_tiles,
    )
    return pl.pallas_call(
        finish,
        out_shape=(
            jax.ShapeDtypeStruct((T, 512), BF16),
            jax.ShapeDtypeStruct((512, 512), F32),
        ),
        in_specs=[vmem, vmem],
        out_specs=(vmem, vmem),
        cost_estimate=pl.CostEstimate(flops=300_000, bytes_accessed=1_900_000, transcendentals=0),
    )(node_t, wgrad)


def solution(mesh):
    return jax.shard_map(
        on_device,
        mesh=mesh,
        in_specs=(
            P(("row", "col", "depth"), None),
            P(("row", "col", "depth"), None),
            P(("row", "col", "depth"), None),
            P(),
            P(("row", "col", "depth"), None, None),
            P(("row", "col", "depth")),
            P(("row", "col", "depth")),
            P(("row", "col", "depth")),
        ),
        out_specs=(P(("row", "col", "depth"), None), P()),
        check_vma=False,
    )
```

```python
import jax
import jax.numpy as jnp
from jax import lax
from jax.experimental import pallas as pl
from jax.experimental.pallas import tpu as pltpu
from jax.sharding import PartitionSpec as P

MESH = pl.DeviceIdType.MESH
F32 = jnp.float32
BF16 = jnp.bfloat16
T = 128
CHUNKS = (128, 128, 128, 128)
NCHUNK = len(CHUNKS)
STARTS = tuple(sum(CHUNKS[:c]) for c in range(NCHUNK))
SLOTS = 84
GROUP = 32
UNROLL = 14
HALF = SLOTS // 2
SEMS = 112


def wrap4(value):
    return lax.rem(value, 4)


class Ring:
    def __init__(self, k, src, unit, rl, rr, fl, fr, out, right, left):
        self.src, self.unit, self.out = src, unit, out
        self.rl, self.rr, self.fl, self.fr = rl, rr, fl, fr
        u = unit
        self.to_right = k.copy(src.at[pl.ds(3 * u, 2 * u)], rl, right)
        self.to_left = k.copy(src.at[pl.ds(5 * u, 2 * u)], rr, left)
        self.sum_right = k.copy(src.at[pl.ds(2 * u, u)], fl, right)
        self.sum_left = k.copy(src.at[pl.ds(7 * u, u)], fr, left)

    def first(self):
        self.to_right.start()
        self.to_left.start()

    def settle(self):
        for sent in (self.to_right, self.to_left, self.sum_right, self.sum_left):
            sent.wait_send()

    def second(self):
        u, src = self.unit, self.src
        self.to_right.wait_recv()
        src[pl.ds(2 * u, u)] = (
            src[pl.ds(2 * u, u)].astype(F32) + self.rl[pl.ds(u, u)].astype(F32)
        ).astype(BF16)
        self.sum_right.start()
        self.to_left.wait_recv()
        src[pl.ds(7 * u, u)] = (
            src[pl.ds(7 * u, u)].astype(F32) + self.rr[pl.ds(0, u)].astype(F32)
        ).astype(BF16)
        self.sum_left.start()

    def last(self):
        u, src = self.unit, self.src
        self.sum_right.wait_recv()
        self.out[pl.ds(0, u)] = (
            src[pl.ds(0, u)].astype(F32)
            + self.fl[...].astype(F32)
            + self.rr[pl.ds(u, u)].astype(F32)
        ).astype(BF16)
        self.sum_left.wait_recv()
        self.out[pl.ds(u, u)] = (
            src[pl.ds(u, u)].astype(F32)
            + self.rl[pl.ds(0, u)].astype(F32)
            + self.fr[...].astype(F32)
        ).astype(BF16)


class Fan:
    def __init__(self, k, src, unit, landed, devices):
        self.src, self.unit, self.landed = src, unit, landed
        self.sends = [
            k.copy(src.at[pl.ds(s * unit, unit)], landed.at[pl.ds((s - 1) * unit, unit)], devices[s - 1])
            for s in (1, 2, 3)
        ]

    def first(self):
        for s in (1, 0, 2):
            self.sends[s].start()

    def settle(self):
        for sent in self.sends:
            sent.wait_send()

    def arrived(self):
        for sent in self.sends:
            sent.wait_recv()

    def total(self):
        u = self.unit
        value = self.src[pl.ds(0, u)].astype(F32)
        for s in range(3):
            value = value + self.landed[pl.ds(s * u, u)].astype(F32)
        return value


class Copies:
    def __init__(self, send_sems, recv_sems):
        self.send_sems, self.recv_sems, self.used = send_sems, recv_sems, 0

    def copy(self, src, dst, device):
        index = self.used
        self.used += 1
        made = pltpu.make_async_remote_copy(
            src_ref=src,
            dst_ref=dst,
            send_sem=self.send_sems.at[index],
            recv_sem=self.recv_sems.at[index],
            device_id=device,
            device_id_type=MESH,
        )
        return made

    def swap(self, src, dst, device):
        sent = self.copy(src, src, device)
        came = pltpu.make_async_remote_copy(
            src_ref=dst,
            dst_ref=dst,
            send_sem=self.send_sems.at[self.used - 1],
            recv_sem=self.recv_sems.at[self.used - 1],
            device_id=device,
            device_id_type=MESH,
        )
        return sent, came


def kernel(
    count_ref, rows_ref, cols_ref, grad_hbm, mask_hbm, agg_hbm, weight_hbm, tiles_hbm,
    node_ref, wgrad_ref,
    grad_v, mask_v, agg_v, weight_v,
    tiles, seg, acc_ref,
    gathered, parts, xl, xr, xfl, xfr, mids, landed, tops, ztop,
    wl, ws, wa, wxd, wb, wyd, wc, wq, wn, wg,
    lists, places, gates, place_s, gate_s,
    send_sems, recv_sems, line_send, line_recv, share_send, share_recv, local_sems,
):
    row, col, depth = lax.axis_index("row"), lax.axis_index("col"), lax.axis_index("depth")
    x, y = lax.div(row, 4), lax.rem(row, 4)
    z, core = lax.div(col, 2), lax.rem(col, 2)
    zz = depth * 8 + z
    quad = lax.rem(z, 4)
    quads = lax.div(zz, 4)

    def device(dx=0, dy=0):
        return (wrap4(x + dx) * 4 + wrap4(y + dy), col, depth)

    def along_z(step):
        place = lax.rem(zz + step, 16)
        return (row, lax.rem(place, 8) * 2 + core, lax.div(place, 8))

    def in_quad(step):
        return (row, (z - quad + wrap4(quad + step)) * 2 + core, depth)

    sibling = (row, z * 2 + 1 - core, depth)
    right_x, left_x = device(dx=1), device(dx=3)
    right_y, left_y = device(dy=1), device(dy=3)
    all_x = [device(dx=s) for s in (1, 2, 3)]
    all_y = [device(dy=s) for s in (1, 2, 3)]
    partner = (row, col, 1 - depth)
    k = Copies(send_sems, recv_sems)

    loads = [
        pltpu.make_async_copy(src, dst, local_sems.at[i])
        for i, (src, dst) in enumerate((
            (grad_hbm, grad_v), (mask_hbm, mask_v), (weight_hbm, weight_v), (agg_hbm, agg_v), (tiles_hbm, tiles),
        ))
    ]
    for load in loads:
        load.start()

    barrier = pltpu.get_barrier_semaphore()
    peers = [sibling] + all_x + all_y + [along_z(s) for s in (1, 15, 2, 14, 4, 8, 12)]
    peers += [in_quad(s) for s in (1, 2, 3)]
    for peer in peers:
        pl.semaphore_signal(barrier, inc=1, device_id=peer, device_id_type=MESH)

    for load in loads[:3]:
        load.wait()
    grad_v[...] = grad_v[...] * mask_v[...].astype(F32).astype(BF16)
    own = core * 8 + z
    for c in range(NCHUNK):
        gathered[c][own] = lax.dot_general(
            weight_v[pl.ds(STARTS[c], CHUNKS[c]), :], grad_v[...], (((1,), (1,)), ((), ())),
            preferred_element_type=F32,
        ).astype(BF16)
    pl.semaphore_wait(barrier, len(peers))

    def there(place):
        return (place >= 0) & (place <= 7)

    def line(c, source, sign, hop, device=None):
        block = gathered[c].at[core * 8 + source]
        return pltpu.make_async_remote_copy(
            src_ref=block, dst_ref=block,
            send_sem=line_send.at[c, source, hop + (1 if sign > 0 else -1)],
            recv_sem=line_recv.at[c, source],
            device_id=device or (row, (z + sign * hop) * 2 + core, depth), device_id_type=MESH,
        )

    def share(c, side):
        half = gathered[c].at[pl.ds(side * 8, 8)]
        return pltpu.make_async_remote_copy(
            src_ref=half, dst_ref=half,
            send_sem=share_send.at[c], recv_sem=share_recv.at[c],
            device_id=sibling, device_id_type=MESH,
        )

    def each_send(c, source, sign, act):
        for hop in (2, 1):
            @pl.when(there(z + sign * hop))
            def _():
                act(line(c, source, sign, hop))

    def begin(c):
        for sign in (1, -1):
            each_send(c, z, sign, lambda made: made.start())

    def forward(c, m):
        for sign in (1, -1):
            source = z - sign * 2 * m

            @pl.when(there(source))
            def _():
                line(c, source, sign, 1, sibling).wait_recv()
                each_send(c, source, sign, lambda made: made.start())

    def deliver(c):
        for m in range(4):
            for sign in (1, -1):
                source = z - sign * (2 * m + 1)

                @pl.when(there(source))
                def _():
                    line(c, source, sign, 1, sibling).wait_recv()
        share(c, core).start()

    def shared(c):
        share(c, 1 - core).wait_recv()

    def line_end(c):
        for m in range(4):
            for sign in (1, -1):
                source = z - sign * 2 * m

                @pl.when(there(source))
                def _():
                    each_send(c, source, sign, lambda made: made.wait_send())
        share(c, core).wait_send()

    w_share = k.copy(wl.at[1 - core], ws, sibling)
    w_x = Fan(k, wa, 256, wxd, all_x)
    w_y = Fan(k, wb, 64, wyd, all_y)
    w_q = [
        k.copy(wc.at[pl.ds(pl.multiple_of(wrap4(quad + s) * 16, 16), 16)], wq.at[s - 1], in_quad(s))
        for s in (1, 2, 3)
    ]
    w_n = [
        k.swap(wn.at[quads], wn.at[wrap4(quads + 4 - s)], along_z(4 * s)) for s in (1, 2, 3)
    ]

    def strip(place):
        return wg.at[core, x, y, pl.ds(pl.multiple_of(place * 16, 16), 16)]

    w_back_q = [k.swap(strip(quad), strip(wrap4(quad + 4 - s)), in_quad(s)) for s in (1, 2, 3)]
    w_back_y = [
        k.swap(wg.at[core, x, y], wg.at[core, x, wrap4(y + 4 - s)], device(dy=s)) for s in (1, 2, 3)
    ]
    w_back_x = [
        k.swap(wg.at[core, x], wg.at[core, wrap4(x + 4 - s)], device(dx=s)) for s in (1, 2, 3)
    ]
    w_back_core = k.swap(wg.at[core], wg.at[1 - core], sibling)

    def weight_0():
        loads[3].wait()
        for h in range(2):
            for q in range(4):
                wl[h, q] = lax.dot_general(
                    agg_v[:, h * 256:(h + 1) * 256], grad_v[:, q * T:(q + 1) * T],
                    (((0,), (0,)), ((), ())), preferred_element_type=F32,
                ).astype(BF16)
        w_share.start()

    def weight_1():
        w_share.wait_recv()
        for a in range(4):
            xt = wrap4(x + a)
            for b in range(4):
                rows = pl.ds(pl.multiple_of(wrap4(y + b) * 64, 64), 64)
                wa[pl.ds(a * 256 + b * 64, 64)] = (
                    wl[core, xt, rows].astype(F32) + ws[xt, rows].astype(F32)
                ).astype(BF16)
        w_x.first()
        w_share.wait_send()

    def weight_2():
        w_x.arrived()
        wb[...] = w_x.total().astype(BF16)
        w_y.first()
        w_x.settle()

    def weight_3():
        w_y.arrived()
        wc[...] = w_y.total().astype(BF16)
        for sent in w_q:
            sent.start()
        w_y.settle()

    def weight_4():
        total = wc[pl.ds(pl.multiple_of(quad * 16, 16), 16)].astype(F32)
        for s in range(3):
            w_q[s].wait_recv()
            total = total + wq[s].astype(F32)
        wn[quads] = total.astype(BF16)
        for sent, _ in w_n:
            sent.start()
        for sent in w_q:
            sent.wait_send()

    def weight_5():
        for _, came in w_n:
            came.wait_recv()
        total = wn[0].astype(F32)
        for place in range(1, 4):
            total = total + wn[place].astype(F32)
        wg[core, x, y, pl.ds(pl.multiple_of(quad * 16, 16), 16)] = total.astype(BF16)
        for sent, _ in w_back_q:
            sent.start()
        for sent, _ in w_n:
            sent.wait_send()

    def weight_6():
        for _, came in w_back_q:
            came.wait_recv()
        for sent, _ in w_back_y:
            sent.start()
        for sent, _ in w_back_q:
            sent.wait_send()

    def weight_7():
        for _, came in w_back_y:
            came.wait_recv()
        for sent, _ in w_back_x:
            sent.start()
        for sent, _ in w_back_y:
            sent.wait_send()

    def weight_8():
        for _, came in w_back_x:
            came.wait_recv()
        w_back_core[0].start()
        for sent, _ in w_back_x:
            sent.wait_send()

    def weight_9():
        w_back_core[1].wait_recv()
        w_back_core[0].wait_send()
        for h in range(2):
            for a in range(4):
                for b in range(4):
                    wgrad_ref[pl.ds(h * 256 + b * 64, 64), a * T:(a + 1) * T] = wg[h, a, b]

    def sort():
        lane = lax.broadcasted_iota(jnp.int32, (1, T), 1)
        lists[...] = jnp.zeros((8, T), jnp.int32)
        lists[0:1, 0:SLOTS] = cols_ref[...]
        lists[1:2, 0:SLOTS] = rows_ref[...]
        key = jnp.where(lane < count_ref[0], lists[0:1, :], GROUP)
        key = jnp.where(lane < SLOTS, key, GROUP)
        tile_row = lists[1:2, :]
        slab_place = (tile_row & 1) * 8 + (tile_row >> 1)
        above = lax.broadcasted_iota(jnp.int32, (T, T), 0)
        across = lax.broadcasted_iota(jnp.int32, (T, T), 1)

        def wide(value):
            return jnp.broadcast_to(value, (T, T))

        def count(mask, value=1):
            return jnp.sum(jnp.where(mask, value, 0), axis=0, keepdims=True)

        key_a = wide(key)
        key_t = key_a.T
        same = (key_t == key_a) & (above < across)
        rank = count((key_t < key_a) | same)
        follows = jnp.minimum(count(same), 1)
        chosen = wide(rank).T == across
        places[0:1, :] = jnp.minimum(count(chosen, above), SLOTS - 1)
        places[1:2, :] = jnp.minimum(count(chosen, wide(slab_place).T), 15)
        places[2:3, :] = jnp.clip(count(key_t <= across) - 1, 0, SLOTS - 1)
        gates[0:1, :] = count(chosen, wide(follows).T).astype(F32)
        gates[1:2, :] = jnp.minimum(count(key_t == across), 1).astype(F32)
        for made in (
            pltpu.make_async_copy(places, place_s, local_sems.at[5]),
            pltpu.make_async_copy(gates, gate_s, local_sems.at[6]),
        ):
            made.start()
            made.wait()

    def compute(c, first, stop):
        width = CHUNKS[c]

        def block(step, acc):
            for inner in range(UNROLL):
                p = first + step * UNROLL + inner
                product = jnp.dot(
                    gathered[c][place_s[1, p]], tiles[place_s[0, p]],
                    preferred_element_type=F32,
                )
                acc = acc * gate_s[0, p] + product
                seg[p, 0:width] = acc.astype(BF16)
            return acc

        if first == 0:
            start = jnp.zeros((width, T), F32)
        else:
            start = acc_ref[0:width]
        end = lax.fori_loop(0, (stop - first) // UNROLL, block, start)
        if stop < SLOTS:
            acc_ref[0:width] = end

    def place(c):
        width = CHUNKS[c]

        def one(m, carry):
            major, minor = lax.div(m, 4), lax.rem(m, 4)
            rows = pl.ds(pl.multiple_of(m * width, width), width)
            for dt in range(2):
                a, b = (major, minor) if dt == 0 else (minor, major)
                target = (wrap4(x + a) * 4 + wrap4(y + b)) * 2 + dt
                parts[c][dt, rows] = (
                    seg[place_s[2, target], 0:width].astype(F32) * gate_s[1, target]
                ).astype(BF16)
            return carry

        lax.fori_loop(0, 16, one, 0)

    ring, fan, cross = [], [], []
    for c in range(NCHUNK):
        for dt in range(2):
            far = (right_x, left_x) if dt == 0 else (right_y, left_y)
            ring.append(Ring(
                k, parts[c].at[dt], 2 * CHUNKS[c],
                xl[c].at[dt], xr[c].at[dt], xfl[c].at[dt], xfr[c].at[dt], mids[c].at[dt], *far,
            ))
            fan.append(Fan(
                k, mids[c].at[dt], CHUNKS[c], landed[c].at[dt], all_y if dt == 0 else all_x
            ))
        cross.append(k.copy(tops[c].at[1 - depth], ztop[c], partner))

    def reduce_1(c):
        for dt in range(2):
            ring[2 * c + dt].first()

    def reduce_2(c):
        for dt in range(2):
            ring[2 * c + dt].second()

    def reduce_3(c):
        for dt in range(2):
            ring[2 * c + dt].last()
            fan[2 * c + dt].first()
        for dt in range(2):
            ring[2 * c + dt].settle()

    def reduce_4(c):
        for dt in range(2):
            fan[2 * c + dt].arrived()
        width = CHUNKS[c]
        for turn, dt in enumerate((1 - depth, depth)):
            total = mids[c][dt, 0:width].astype(F32)
            for s in range(3):
                total = total + landed[c][dt, s * width:(s + 1) * width].astype(F32)
            tops[c][dt] = total.astype(BF16)
            if turn == 0:
                cross[c].start()
        for dt in range(2):
            fan[2 * c + dt].settle()

    def reduce_5(c):
        cross[c].wait_send()
        cross[c].wait_recv()
        node_ref[pl.ds(STARTS[c], CHUNKS[c])] = (
            tops[c][depth].astype(F32) + ztop[c][...].astype(F32)
        ).astype(BF16)

    begin(0)
    begin(1)
    sort()
    begin(2)
    weight_0()
    forward(0, 1)
    forward(1, 1)
    forward(2, 1)
    forward(0, 2)
    forward(1, 2)
    forward(2, 2)
    forward(0, 3)
    weight_1()
    begin(3)
    forward(1, 3)
    forward(2, 3)
    deliver(0)
    forward(3, 1)
    weight_2()
    shared(0)
    loads[4].wait()
    compute(0, 0, HALF)
    deliver(1)
    compute(0, HALF, SLOTS)
    deliver(2)
    forward(3, 2)
    shared(1)
    place(0)
    reduce_1(0)
    compute(1, 0, HALF)
    compute(1, HALF, SLOTS)
    place(1)
    reduce_1(1)
    forward(3, 3)
    shared(2)
    compute(2, 0, HALF)
    reduce_2(0)
    weight_3()
    line_end(2)
    compute(2, HALF, SLOTS)
    deliver(3)
    place(2)
    reduce_1(2)
    weight_4()
    reduce_2(1)
    reduce_3(0)
    shared(3)
    compute(3, 0, HALF)
    compute(3, HALF, SLOTS)
    place(3)
    reduce_1(3)
    reduce_2(2)
    line_end(3)
    reduce_3(1)
    line_end(0)
    reduce_4(0)
    weight_5()
    line_end(1)
    reduce_2(3)
    reduce_3(2)
    reduce_4(1)
    weight_6()
    reduce_3(3)
    reduce_5(0)
    reduce_4(2)
    weight_7()
    reduce_4(3)
    reduce_5(1)
    weight_8()
    weight_9()
    reduce_5(2)
    reduce_5(3)


def finish(node_t_ref, wgrad_t_ref, node_ref, wgrad_ref):
    for q in range(4):
        node_ref[:, q * T:(q + 1) * T] = node_t_ref[q * T:(q + 1) * T].astype(F32).T.astype(BF16)
    wgrad_ref[...] = wgrad_t_ref[...].astype(F32)


def on_device(
    grad_out, relu_mask, aggregated, weight, adjacency_tiles, tile_rows, tile_cols, tile_count
):
    smem = pl.BlockSpec(memory_space=pltpu.SMEM)
    vmem = pl.BlockSpec(memory_space=pltpu.VMEM)
    hbm = pl.BlockSpec(memory_space=pltpu.HBM)
    bf = lambda *shape: pltpu.VMEM(shape, BF16)
    each = lambda make: tuple(make(width) for width in CHUNKS)
    two = lambda times: each(lambda width: bf(2, times * width, T))
    node_t, wgrad = pl.pallas_call(
        kernel,
        out_shape=(
            jax.ShapeDtypeStruct((512, T), BF16),
            jax.ShapeDtypeStruct((512, 512), BF16),
        ),
        in_specs=[smem, vmem, vmem, hbm, hbm, hbm, hbm, hbm],
        out_specs=(vmem, vmem),
        scratch_shapes=[
            bf(T, 512), pltpu.VMEM((T, 512), jnp.int32), bf(T, 512), bf(512, 512),
            bf(SLOTS, T, T), bf(SLOTS, T, T), pltpu.VMEM((T, T), F32),
            each(lambda width: bf(16, width, T)),
            two(16), two(4), two(4), two(2), two(2), two(4), two(3), two(1),
            each(lambda width: bf(width, T)),
            bf(2, 4, 256, T), bf(4, 256, T), bf(1024, T), bf(768, T),
            bf(256, T), bf(192, T),
            bf(64, T), bf(3, 16, T), bf(4, 16, T), bf(2, 4, 4, 64, T),
            pltpu.VMEM((8, T), jnp.int32), pltpu.VMEM((8, T), jnp.int32), pltpu.VMEM((8, T), F32),
            pltpu.SMEM((8, T), jnp.int32), pltpu.SMEM((8, T), F32),
            pltpu.SemaphoreType.DMA((SEMS,)),
            pltpu.SemaphoreType.DMA((SEMS,)),
            pltpu.SemaphoreType.DMA((NCHUNK, 8, 4)),
            pltpu.SemaphoreType.DMA((NCHUNK, 8)),
            pltpu.SemaphoreType.DMA((NCHUNK,)),
            pltpu.SemaphoreType.DMA((NCHUNK,)),
            pltpu.SemaphoreType.DMA((7,)),
        ],
        compiler_params=pltpu.CompilerParams(
            collective_id=0, has_side_effects=True, vmem_limit_bytes=60 * 1024 * 1024
        ),
        cost_estimate=pl.CostEstimate(flops=1_600_000_000, bytes_accessed=5_000_000, transcendentals=0),
    )(
        tile_count, tile_rows.reshape(1, SLOTS), tile_cols.reshape(1, SLOTS),
        grad_out, relu_mask, aggregated, weight, adjacency_tiles,
    )
    return pl.pallas_call(
        finish,
        out_shape=(
            jax.ShapeDtypeStruct((T, 512), BF16),
            jax.ShapeDtypeStruct((512, 512), F32),
        ),
        in_specs=[vmem, vmem],
        out_specs=(vmem, vmem),
        cost_estimate=pl.CostEstimate(flops=300_000, bytes_accessed=1_900_000, transcendentals=0),
    )(node_t, wgrad)


def solution(mesh):
    return jax.shard_map(
        on_device,
        mesh=mesh,
        in_specs=(
            P(("row", "col", "depth"), None),
            P(("row", "col", "depth"), None),
            P(("row", "col", "depth"), None),
            P(),
            P(("row", "col", "depth"), None, None),
            P(("row", "col", "depth")),
            P(("row", "col", "depth")),
            P(("row", "col", "depth")),
        ),
        out_specs=(P(("row", "col", "depth"), None), P()),
        check_vma=False,
    )
```
